256 devices in a mesh: section: 2 (over x_lo), ctx: 32 (over z, x_hi, core), head: 4 (over y).
Axes of the slice: x: 4 (x_hi: 2, x_lo: 2; x = x_hi * 2 + x_lo), y: 4, z: 8, core: 2. Of those that a mesh axis runs over, the one named last changes fastest.
Arguments:
- latent: bfloat16 [2, 4096, 576], P('section', 'ctx'), may hold values from -5 to 5
- queries: bfloat16 [2, 4096, 12288], P('section', 'ctx', 'head'), may hold values from -300 to 300
- w_key: bfloat16 [2, 512, 8192], P('section', None, 'head'), may hold values from -0.25 to 0.25
- w_value: bfloat16 [2, 512, 8192], P('section', None, 'head'), may hold values from -1 to 1
- w_next: bfloat16 [2, 8192, 576], P('section', 'head'), may hold values from -0.0625 to 0.0625
- segments: int32 [2, 4096], P('section', 'ctx'), may hold values from 0 to 3, never falling along the last dimension, each value on 1 to 2048 neighbouring positions
Outputs:
- attention: bfloat16 [2, 4096, 8192], P('section', 'ctx', 'head')
- next_latent: bfloat16 [2, 4096, 576], P('section', 'ctx')
The draws below stay inside these ranges and needn't reach their ends.
Inputs may be any that keep to these rules, and one draw needn't show every extreme that they name: `segments`: document numbers never fall along a sequence; each sequence holds 4 documents, and one of them has half of its 4096 tokens.
All inputs are finite; a program needn't handle non-finite values.
Results may differ from the reference program's by a relative error of at most 0.017.
Values may be sent and summed in bfloat16 or wider, within the bound.
A program may use at most 192 MiB of HBM per device.

```python
import math
import jax
import jax.numpy as jnp
import numpy as np
from jax import lax

HEADS = 64
KV_RANK = 512
ROPE = 64
NOPE = 128
VDIM = 128
DOCS = 4
SEQ = 4096
LAT = 576


def shared_rope(key):
    return jnp.clip(jax.random.normal(jax.random.fold_in(key, 17), (2, SEQ, ROPE), jnp.float32), -4.0, 4.0)


def draw_latent(key, part):
    rope_part = shared_rope(key)
    key = jax.random.fold_in(key, 3)
    compressed = jnp.clip(jax.random.normal(key, (2, SEQ, KV_RANK), jnp.float32), -5.0, 5.0)
    return jnp.concatenate([compressed, rope_part], axis=2).astype(jnp.bfloat16)


def draw_queries(key, part):
    key = jax.random.fold_in(key, 4)
    head_width = NOPE + ROPE
    sample_values = 1.5 * jnp.clip(jax.random.normal(key, (2, SEQ, HEADS, head_width), jnp.float32), -6.0, 6.0)
    return sample_values.reshape(2, SEQ, HEADS * head_width).astype(jnp.bfloat16)


def block_scale(key, extent, shards, least, top_value):
    loudness, own = 1.0, jax.random.fold_in(key, 6)
    for position, shards_of in shards:
        steps = jnp.exp(jax.random.uniform(jax.random.fold_in(own, position), (shards_of,), jnp.float32, least / len(shards), top_value / len(shards)))
        loudness = loudness * jnp.repeat(steps, extent[position] // shards_of).reshape([-1 if axis == position else 1 for axis in range(len(extent))])
    return loudness


def length_profile(amount, total, most, slope):
    weights = [(1 << 20) // math.isqrt(standing ** slope) + 1 for standing in range(2, amount + 1)]
    surplus, holding = total - most - (amount - 1), [1] * (amount - 1)
    while surplus > 0:
        free = [i for i in range(amount - 1) if holding[i] < most]
        mass, left = sum([weights[i] for i in free]), surplus
        for i in free:
            extra = min(most - holding[i], max(1, left * weights[i] // mass), surplus)
            holding[i] = holding[i] + extra
            surplus = surplus - extra
    return np.array([most] + holding)


def uneven_parts(own_key, amount, total, reach, skew):
    if amount == 2:
        one = jax.random.randint(own_key, (), max(1, total - reach), min(reach, total - 1) + 1)
        return jnp.stack([one, total - one])
    lengths = jnp.asarray(length_profile(amount, total, reach, skew), jnp.int32)
    twos = (amount - 1) // 2
    giver, receiver = lengths[1:1 + 2 * twos:2], lengths[2:2 + 2 * twos:2]
    margin = jnp.minimum(giver - 1, reach - receiver)
    passed = jax.random.randint(jax.random.fold_in(own_key, 1), (twos,), 0, 1 << 20) % (margin + 1)
    lengths = lengths.at[1:1 + 2 * twos:2].set(giver - passed).at[2:2 + 2 * twos:2].set(receiver + passed)
    return lengths[jax.random.permutation(jax.random.fold_in(own_key, 2), amount)]


def gaussian(stream_key, shape, scale, most, shards=(), kind=jnp.bfloat16):
    values = scale * jax.random.normal(stream_key, shape, jnp.float32)
    if shards:
        values = values * block_scale(stream_key, shape, shards, -0.22, 0.18)
    return jnp.clip(values, -most, most).astype(kind)


def setup_inputs(seed: int = 0) -> dict:
    keys = jax.random.split(jax.random.key(seed), 7)
    return {
        "latent": draw_latent(jax.random.fold_in(keys[6], 71), 0),
        "queries": draw_queries(jax.random.fold_in(keys[6], 71), 0),
        "w_key": gaussian(keys[2], (2, KV_RANK, HEADS * NOPE), KV_RANK ** -0.5, 0.25, ((0, 2), (2, 4))),
        "w_value": gaussian(keys[3], (2, KV_RANK, HEADS * VDIM), (KV_RANK // 16) ** -0.5, 1.0, ((0, 2), (2, 4))),
        "w_next": gaussian(keys[4], (2, HEADS * VDIM, LAT), (HEADS * VDIM) ** -0.5, 0.0625, ((0, 2), (1, 4))),
        "segments": jax.vmap(lambda own: jnp.searchsorted(jnp.cumsum(uneven_parts(own, DOCS, SEQ, SEQ // 2, 0)), jnp.arange(SEQ), side="right"))(jax.random.split(keys[5], 2)).reshape((2, SEQ)).astype(jnp.int32),
    }


def attend_section(latent_rows, query_rows, key_weight, value_weight, doc_ids):
    compressed = latent_rows[:, :KV_RANK]
    rope_key = latent_rows[:, KV_RANK:]
    keys_nope = jnp.dot(compressed, key_weight, preferred_element_type=jnp.float32).astype(jnp.bfloat16)
    values = jnp.dot(compressed, value_weight, preferred_element_type=jnp.float32).astype(jnp.bfloat16)
    head_width = NOPE + ROPE
    query_heads = query_rows.reshape(SEQ, HEADS, head_width)
    key_heads = keys_nope.reshape(SEQ, HEADS, NOPE)
    value_heads = values.reshape(SEQ, HEADS, VDIM)
    positions = jnp.arange(SEQ, dtype=jnp.int32)
    allowed = (positions[None, :] <= positions[:, None]) & (doc_ids[None, :] == doc_ids[:, None])
    score_scale = 1.0 / math.sqrt(head_width)

    def one_head(head_index):
        query_head = query_heads[:, head_index, :]
        key_head = key_heads[:, head_index, :]
        value_head = value_heads[:, head_index, :]
        scores = jnp.dot(query_head[:, :NOPE], key_head.T, preferred_element_type=jnp.float32)
        scores = scores + jnp.dot(query_head[:, NOPE:], rope_key.T, preferred_element_type=jnp.float32)
        scores = scores * score_scale
        row_max = lax.optimization_barrier(jnp.max(jnp.where(allowed, scores, -jnp.inf), axis=1))
        exponents = jnp.where(allowed, jnp.exp(scores - row_max[:, None]), 0.0)
        denominator = lax.optimization_barrier(jnp.sum(exponents, axis=1))
        weights = exponents.astype(jnp.bfloat16)
        return jnp.dot(weights, value_head, preferred_element_type=jnp.float32) / denominator[:, None]
    outputs = lax.map(one_head, jnp.arange(HEADS, dtype=jnp.int32))
    return jnp.transpose(outputs, (1, 0, 2)).reshape(SEQ, HEADS * VDIM).astype(jnp.bfloat16)

def project_next(attention_rows, next_weight):
    projected = jnp.dot(attention_rows, next_weight, preferred_element_type=jnp.float32)
    compressed = projected[:, :KV_RANK]
    inverse = lax.rsqrt(lax.optimization_barrier(jnp.mean(compressed * compressed, axis=1, keepdims=True)) + 1e-06)
    return jnp.concatenate([compressed * inverse, projected[:, KV_RANK:]], axis=1).astype(jnp.bfloat16)

def reference(latent, queries, w_key, w_value, w_next, segments):
    first_layer = attend_section(latent[0], queries[0], w_key[0], w_value[0], segments[0])
    second_layer = attend_section(latent[1], queries[1], w_key[1], w_value[1], segments[1])
    attention = jnp.stack([first_layer, second_layer])
    next_latent = jnp.stack([project_next(second_layer, w_next[1]), project_next(first_layer, w_next[0])])
    return (attention, next_latent)
```

```python
import math

import jax
import jax.numpy as jnp
from jax import lax
from jax.experimental import pallas as pl
from jax.experimental.pallas import tpu as pltpu
from jax.sharding import PartitionSpec as P

MESH = pl.DeviceIdType.MESH
RANK = 512
ROPE = 64
NOPE = 128
VDIM = 128
LAT = 576
WIDE = 640
ROWS = 128
QUARTER = 32
CHUNK = 512
CHUNKS = 4
KEYS = ROWS + CHUNK * CHUNKS
DOCS = 4
BIG = float(2**30)
FOLD = math.log2(math.e) / math.sqrt(NOPE + ROPE)
NT = (((1,), (1,)), ((), ()))
F32 = jnp.float32
BF16 = jnp.bfloat16
X0, Z1A, Z1B, SIB, Z, YL, YR, FL, FR, CORE, RS, NL, SEMS = 0, 1, 2, 3, 4, 8, 12, 16, 20, 24, 28, 31, 35


def make_kernel(planes, heads):
    rows_all = heads * ROWS
    group = 4
    grow = group * ROWS
    groups = heads // group

    def kernel(lat_hbm, q_hbm, wk_hbm, wv_hbm, wn_hbm, seg_hbm, att_hbm, next_hbm,
               lat, seg, qv, wk, wv, wn, qx, kx, xp, sib, sc, top, ob, att, proj, part, rsb, nlp, nlb,
               ls, ss, rs):
        s = lax.axis_index("section")
        t = lax.axis_index("ctx")
        y = lax.axis_index("head")
        z, xh, c = t // 4, (t // 2) % 2, t % 2

        def at(zz, xx, cc, yy, section=s):
            return {"section": section, "ctx": zz * 4 + xx * 2 + cc, "head": yy}

        up, down = (z + 1) % planes, (z + planes - 1) % planes
        right, left, across = (y + 1) % 4, (y + 3) % 4, (y + 2) % 4

        def load(i, src, dst):
            return pltpu.make_async_copy(src, dst, ls.at[i])

        loads = [
            load(0, lat_hbm.at[0], lat),
            load(1, seg_hbm, seg),
            load(2, q_hbm.at[0], qv),
            load(3, wk_hbm.at[0], wk),
            load(4, wv_hbm.at[0], wv),
            load(5, wn_hbm.at[0], wn),
        ]
        for one in loads:
            one.start()

        barrier = pltpu.get_barrier_semaphore()
        peers = [
            at(down, xh, c, y), at(down, 1 - xh, c, y), at(z, 1 - xh, c, y), at(z, xh, 1 - c, y),
            at(z, xh, c, right), at(z, xh, c, left), at(z, xh, c, across),
        ] + [at(z, xh, c, (y + d) % 4, 1 - s) for d in range(4)]
        for peer in peers:
            pl.semaphore_signal(barrier, inc=1, device_id=peer, device_id_type=MESH)

        def remote(i, src, dst, peer):
            return pltpu.make_async_remote_copy(
                src_ref=src, dst_ref=dst, send_sem=ss.at[i], recv_sem=rs.at[i], device_id=peer, device_id_type=MESH
            )

        sent = []

        def send(i, src, dst, peer):
            one = remote(i, src, dst, peer)
            one.start()
            sent.append(one)

        def arrive(i, dst):
            remote(i, dst, dst, at(z, xh, c, right)).wait_recv()

        def rows(start, size):
            return kx.at[pl.ds(pl.multiple_of(start, QUARTER), size)]

        def pair(k, yy):
            return rows(ROWS + CHUNK * (k - 1) + c * 256 + yy * 64, 64)

        def piece(k, yy, xx):
            return rows(ROWS + CHUNK * (k - 1) + c * 256 + yy * 64 + xx * QUARTER, QUARTER)

        def half(k, cc):
            return rows(ROWS + CHUNK * (k - 1) + cc * 256, 256)

        loads[0].wait()
        loads[1].wait()
        lane = lax.broadcasted_iota(jnp.int32, (ROWS, 128), 1)
        doc = jnp.broadcast_to(seg[...].astype(F32), (ROWS, 128)).T
        slot = (lane - ROPE).astype(F32)
        in_slot = (lane >= ROPE) & (lane < ROPE + DOCS)
        mine = in_slot & (slot == doc)
        kx[0:ROWS, 0:RANK] = lat[:, 0:RANK]
        rope = jnp.concatenate([lat[:, RANK:LAT].astype(F32), jnp.zeros((ROWS, ROPE), F32)], axis=1)
        kx[0:ROWS, RANK:WIDE] = jnp.where(mine, 1.0, rope).astype(BF16)
        q_mark = jnp.where(in_slot & (slot != doc), -BIG, 0.0)
        pl.semaphore_wait(barrier, len(peers))

        own = rows(y * QUARTER, QUARTER)
        send(Z1A, own, piece(1, y, xh), at(up, xh, c, y))
        send(Z1B, own, piece(1, y, xh), at(up, 1 - xh, c, y))
        send(X0, own, xp, at(z, 1 - xh, c, y))
        send(SIB, kx.at[pl.ds(0, ROWS)], sib, at(z, xh, 1 - c, y))

        def stage_z(k):
            if k == 1:
                arrive(Z1A, piece(1, y, xh))
                arrive(Z1B, piece(1, y, 1 - xh))
            else:
                arrive(Z + k - 1, pair(k, y))
            start = pl.multiple_of(ROWS + CHUNK * (k - 1) + c * 256 + y * 64, 64)

            @pl.when(z < k)
            def _():
                mark = lax.broadcasted_iota(jnp.int32, (64, 128), 1)
                kx[pl.ds(start, 64), RANK:WIDE] = jnp.where(
                    (mark >= ROPE) & (mark < ROPE + DOCS), 1.0, 0.0
                ).astype(BF16)

            if k == CHUNKS:
                arrive(X0, xp)

                @pl.when(xh == 1)
                def _():
                    kx[pl.ds(start, QUARTER), :] = xp[...]
            else:
                send(Z + k, pair(k, y), pair(k + 1, y), at(up, xh, c, y))
            send(YL + k - 1, pair(k, y), pair(k, y), at(z, xh, c, right))
            send(YR + k - 1, pair(k, y), pair(k, y), at(z, xh, c, left))

        def stage_y(k):
            arrive(YL + k - 1, pair(k, left))
            send(FL + k - 1, piece(k, left, 0), piece(k, left, 0), at(z, xh, c, right))
            arrive(YR + k - 1, pair(k, right))
            send(FR + k - 1, piece(k, right, 1), piece(k, right, 1), at(z, xh, c, left))

        def stage_f(k):
            arrive(FL + k - 1, piece(k, across, 0))
            arrive(FR + k - 1, piece(k, across, 1))
            send(CORE + k - 1, half(k, c), half(k, c), at(z, xh, 1 - c, y))

        def stage_c(k):
            arrive(CORE + k - 1, half(k, 1 - c))
            if k == CHUNKS:
                arrive(SIB, sib)

                @pl.when(c == 1)
                def _():
                    for yy in range(4):
                        start = pl.multiple_of(ROWS + CHUNK * (k - 1) + yy * 64 + xh * QUARTER, QUARTER)
                        kx[pl.ds(start, QUARTER), :] = sib[yy * QUARTER : (yy + 1) * QUARTER, :]

        def queries(p):
            base = 3 * 128 * p
            one = qv[:, base : base + 128]
            two = qv[:, base + 128 : base + 256].astype(F32)
            three = qv[:, base + 256 : base + 384].astype(F32)
            two_turned = pltpu.roll(two, 64, 1)
            three_turned = pltpu.roll(three, 64, 1)
            second = jnp.where(lane < 64, two_turned, three_turned).astype(BF16)
            for h, nope, pos in ((2 * p, one, two), (2 * p + 1, second, three_turned)):
                absorbed = lax.dot_general(
                    nope, wk[:, h * NOPE : (h + 1) * NOPE], NT, preferred_element_type=F32
                )
                qx[h * ROWS : (h + 1) * ROWS, 0:RANK] = (absorbed * FOLD).astype(BF16)
                qx[h * ROWS : (h + 1) * ROWS, RANK:WIDE] = jnp.where(lane < ROPE, pos * FOLD, q_mark).astype(BF16)

        def lane_max(scores):
            best = scores[:, 0:128]
            for i in range(1, scores.shape[1] // 128):
                best = jnp.maximum(best, scores[:, i * 128 : (i + 1) * 128])
            return best

        def diagonal():
            later = lax.broadcasted_iota(jnp.int32, (ROWS, ROWS), 1) > lax.broadcasted_iota(
                jnp.int32, (ROWS, ROWS), 0
            )
            mask = jnp.concatenate([jnp.where(later, -2.0 * BIG, 0.0)] * group, axis=0)
            for g in range(groups):
                r = slice(g * grow, (g + 1) * grow)
                scores = lax.dot_general(qx[r, :], kx[0:ROWS, :], NT, preferred_element_type=F32)
                scores = scores + mask
                sc[r, 0:ROWS] = scores
                top[r, :] = scores

        def chunk_scores(k, g):
            r = slice(g * grow, (g + 1) * grow)
            first = ROWS + CHUNK * (k - 1)
            scores = lax.dot_general(qx[r, :], kx[first : first + CHUNK, :], NT, preferred_element_type=F32)
            sc[r, first : first + CHUNK] = scores
            top[r, :] = jnp.maximum(top[r, :], lane_max(scores))

        def lane_sum(weights):
            total = weights[:, 0:128]
            for i in range(1, weights.shape[1] // 128):
                total = total + weights[:, i * 128 : (i + 1) * 128]
            return total

        def finish(g):
            r = slice(g * grow, (g + 1) * grow)
            first = KEYS - CHUNK
            last = lax.dot_general(qx[r, :], kx[first:KEYS, :], NT, preferred_element_type=F32)
            high = jnp.max(jnp.maximum(top[r, :], lane_max(last)), axis=1, keepdims=True)
            early = jnp.exp2(sc[r, :] - high)
            late = jnp.exp2(last - high)
            total = jnp.sum(lane_sum(early) + lane_sum(late), axis=1, keepdims=True)
            mixed = jnp.dot(early.astype(BF16), kx[0:first, 0:RANK], preferred_element_type=F32)
            mixed = mixed + jnp.dot(late.astype(BF16), kx[first:KEYS, 0:RANK], preferred_element_type=F32)
            ob[r, :] = (mixed * (1.0 / total)).astype(BF16)
            for h in range(g * group, (g + 1) * group):
                att[:, h * VDIM : (h + 1) * VDIM] = jnp.dot(
                    ob[h * ROWS : (h + 1) * ROWS, :],
                    wv[:, h * VDIM : (h + 1) * VDIM],
                    preferred_element_type=F32,
                ).astype(BF16)

        half_pairs = heads // 4
        loads[2].wait()
        loads[3].wait()
        for p in range(half_pairs):
            queries(p)
        stage_z(1)
        for p in range(half_pairs, 2 * half_pairs):
            queries(p)
        diagonal()
        stage_y(1)
        stage_z(2)
        stage_f(1)
        stage_y(2)
        stage_z(3)
        stage_c(1)
        for g in range(groups):
            chunk_scores(1, g)
            if g == 1:
                stage_f(2)
        stage_y(3)
        stage_z(4)
        stage_c(2)
        for g in range(groups):
            chunk_scores(2, g)
            if g == 1:
                stage_f(3)
        stage_y(4)
        stage_c(3)
        for g in range(groups):
            chunk_scores(3, g)
            if g == 1:
                stage_f(4)
        stage_c(4)
        loads[4].wait()
        for g in range(groups):
            finish(g)
        store = pltpu.make_async_copy(att, att_hbm.at[0], ls.at[6])
        store.start()
        loads[5].wait()
        proj[...] = jnp.dot(att[...], wn[...], preferred_element_type=F32)
        part[...] = proj[...].astype(BF16)
        for d in range(1, 4):
            to = (y + d) % 4
            send(
                RS + d - 1,
                part.at[pl.ds(pl.multiple_of(to * QUARTER, QUARTER), QUARTER)],
                rsb.at[d - 1],
                at(z, xh, c, to),
            )
        total = proj[pl.ds(pl.multiple_of(y * QUARTER, QUARTER), QUARTER), :]
        for d in range(1, 4):
            arrive(RS + d - 1, rsb.at[d - 1])
            total = total + rsb[d - 1].astype(F32)
        low = total[:, 0:RANK]
        inverse = lax.rsqrt(jnp.sum(low * low, axis=1, keepdims=True) * (1.0 / RANK) + 1e-06)
        nlp[:, 0:RANK] = (low * inverse).astype(BF16)
        nlp[:, RANK:LAT] = total[:, RANK:LAT].astype(BF16)

        def block(yy):
            return nlb.at[pl.ds(pl.multiple_of(yy * QUARTER, QUARTER), QUARTER)]

        for d in range(4):
            send(NL + d, nlp, block(y), at(z, xh, c, (y + d) % 4, 1 - s))
        for d in range(4):
            arrive(NL + d, block((y + 4 - d) % 4))
        out = pltpu.make_async_copy(nlb, next_hbm.at[0], ls.at[7])
        out.start()
        for one in sent:
            one.wait_send()
        store.wait()
        out.wait()

    def call(latent, queries, w_key, w_value, w_next, segments):
        return pl.pallas_call(
            kernel,
            out_shape=(
                jax.ShapeDtypeStruct((1, ROWS, heads * VDIM), BF16),
                jax.ShapeDtypeStruct((1, ROWS, LAT), BF16),
            ),
            in_specs=[pl.BlockSpec(memory_space=pl.ANY)] * 6,
            out_specs=[pl.BlockSpec(memory_space=pl.ANY)] * 2,
            scratch_shapes=[
                pltpu.VMEM((ROWS, LAT), BF16),
                pltpu.VMEM((1, ROWS), jnp.int32),
                pltpu.VMEM((ROWS, heads * (NOPE + ROPE)), BF16),
                pltpu.VMEM((RANK, heads * NOPE), BF16),
                pltpu.VMEM((RANK, heads * VDIM), BF16),
                pltpu.VMEM((heads * VDIM, LAT), BF16),
                pltpu.VMEM((rows_all, WIDE), BF16),
                pltpu.VMEM((KEYS, WIDE), BF16),
                pltpu.VMEM((QUARTER, WIDE), BF16),
                pltpu.VMEM((ROWS, WIDE), BF16),
                pltpu.VMEM((rows_all, KEYS - CHUNK), F32),
                pltpu.VMEM((rows_all, 128), F32),
                pltpu.VMEM((rows_all, RANK), BF16),
                pltpu.VMEM((ROWS, heads * VDIM), BF16),
                pltpu.VMEM((ROWS, LAT), F32),
                pltpu.VMEM((ROWS, LAT), BF16),
                pltpu.VMEM((3, QUARTER, LAT), BF16),
                pltpu.VMEM((QUARTER, LAT), BF16),
                pltpu.VMEM((ROWS, LAT), BF16),
                pltpu.SemaphoreType.DMA((8,)),
                pltpu.SemaphoreType.DMA((SEMS,)),
                pltpu.SemaphoreType.DMA((SEMS,)),
            ],
            compiler_params=pltpu.CompilerParams(
                collective_id=0, has_side_effects=True, vmem_limit_bytes=58 * 2**20
            ),
            name="attend",
        )(latent, queries, w_key, w_value, w_next, segments)

    return call


def solution(mesh):
    planes = mesh.shape["ctx"] // 4

    def local(latent, queries, w_key, w_value, w_next, segments):
        return make_kernel(planes, w_key.shape[2] // NOPE)(latent, queries, w_key, w_value, w_next, segments)

    in_specs = (
        P("section", "ctx", None),
        P("section", "ctx", "head"),
        P("section", None, "head"),
        P("section", None, "head"),
        P("section", "head", None),
        P("section", "ctx"),
    )
    out_specs = (P("section", "ctx", "head"), P("section", "ctx", None))
    return jax.shard_map(local, mesh=mesh, in_specs=in_specs, out_specs=out_specs, check_vma=False)
```

```python
import math

import jax
import jax.numpy as jnp
from jax import lax
from jax.experimental import pallas as pl
from jax.experimental.pallas import tpu as pltpu
from jax.sharding import PartitionSpec as P

MESH = pl.DeviceIdType.MESH
RANK = 512
ROPE = 64
NOPE = 128
VDIM = 128
LAT = 576
WIDE = 640
ROWS = 128
QUARTER = 32
HALF = 16
CHUNK = 512
CHUNKS = 4
KEYS = ROWS + CHUNK * CHUNKS
DOCS = 4
BIG = float(2**30)
FOLD = math.log2(math.e) / math.sqrt(NOPE + ROPE)
NT = (((1,), (1,)), ((), ()))
F32 = jnp.float32
BF16 = jnp.bfloat16
SEMS = 72
ROUTES = ('', 'X', 'D', 'X', 'S')
PLAN = (
    ("q", 0), ("q", 1), ("q", 2), ("q", 3), ("q", 4), ("z", 1), ("q", 5), ("q", 6), ("q", 7), ("z", 2),
    ("diag", 0), ("diag", 1), ("diag", 2), ("diag", 3), ("xs", 1, 1), ("xs", 1, 3), ("z", 3), ("xs", 1, 2),
    ("ca", 1), ("x", 2), ("z", 4), ("ca", 2), ("xs", 3, 1), ("xs", 3, 3), ("xs", 3, 2), ("ca", 3), ("cb", 1),
    ("cb", 2), ("done", 1), ("qk", 1, 0), ("qk", 1, 1), ("done", 2), ("qk", 1, 2), ("ca", 4), ("qk", 1, 3),
    ("qk", 2, 0), ("cb", 4), ("qk", 2, 1), ("qk", 2, 2), ("qk", 2, 3), ("cb", 3), ("done", 3), ("qk", 3, 0),
    ("qk", 3, 1), ("qk", 3, 2), ("qk", 3, 3), ("done", 4),
)


def make_kernel(planes, heads):
    rows_all = heads * ROWS
    group = 4
    grow = group * ROWS
    groups = heads // group
    ids = {}

    def kernel(lat_hbm, q_hbm, wk_hbm, wv_hbm, wn_hbm, seg_hbm, att_hbm, next_hbm,
               lat, seg, qv, wk, wv, wn, qx, kx, sc, top, ob, att, proj, part, rsa, rsb, nla, nlb,
               ls, ss, rs, ready):
        s = lax.axis_index("section")
        t = lax.axis_index("ctx")
        y = lax.axis_index("head")
        z, xh, c = t // 4, (t // 2) % 2, t % 2

        def at(zz, xx, cc, yy, section=s):
            return {"section": section, "ctx": zz * 4 + xx * 2 + cc, "head": yy}

        right, left, across = (y + 1) % 4, (y + 3) % 4, (y + 2) % 4

        def load(i, src, dst):
            return pltpu.make_async_copy(src, dst, ls.at[i])

        loads = [
            load(0, lat_hbm.at[0], lat),
            load(1, seg_hbm, seg),
            load(2, q_hbm.at[0], qv),
            load(3, wk_hbm.at[0], wk),
            load(4, wv_hbm.at[0], wv),
            load(5, wn_hbm.at[0], wn),
        ]
        for one in loads:
            one.start()

        barrier = pltpu.get_barrier_semaphore()
        peers = [at(z, xh, 1 - c, y), at(z, 1 - xh, c, y)]
        peers += [at(z, xx, c, yy) for xx in (xh, 1 - xh) for yy in (right, left, across)]
        peers += [at(z, xh, c, (y + d) % 4, 1 - s) for d in range(4)]
        for peer in peers:
            pl.semaphore_signal(barrier, inc=1, device_id=peer, device_id_type=MESH)
        for k in (1, 2):

            @pl.when(z + k < planes)
            def _():
                pl.semaphore_signal(barrier, inc=1, device_id=at((z + k) % planes, xh, c, y), device_id_type=MESH)

        @pl.when(z >= 1)
        def _():
            pl.semaphore_signal(barrier, inc=1, device_id=at((z + planes - 1) % planes, xh, c, y), device_id_type=MESH)

        def remote(name, src, dst, peer):
            i = ids.setdefault(name, len(ids))
            return pltpu.make_async_remote_copy(
                src_ref=src, dst_ref=dst, send_sem=ss.at[i], recv_sem=rs.at[i], device_id=peer, device_id_type=MESH
            )

        sent = []

        def send(name, src, dst, peer, when=None):
            one = remote(name, src, dst, peer)
            if when is None:
                one.start()
            else:
                pl.when(when)(one.start)
            sent.append((when, one))

        def arrive(name, dst, when=None):
            wait = remote(name, dst, dst, at(z, xh, c, right)).wait_recv
            if when is None:
                wait()
            else:
                pl.when(when)(wait)

        def start_of(k, cc, xx, yy=0):
            return pl.multiple_of(ROWS + CHUNK * (k - 1) + cc * 256 + xx * ROWS + yy * QUARTER, QUARTER)

        def block(k, cc, xx):
            return kx.at[pl.ds(start_of(k, cc, xx), ROWS)]

        def piece(k, xx, yy):
            return kx.at[pl.ds(start_of(k, c, xx, yy), QUARTER)]

        def beside(yy):
            return at(z, xh, c, yy)

        partner, twin = at(z, 1 - xh, c, y), at(z, xh, 1 - c, y)
        own = kx.at[pl.ds(0, ROWS)]
        own_piece = kx.at[pl.ds(pl.multiple_of(y * QUARTER, QUARTER), QUARTER)]

        loads[0].wait()
        loads[1].wait()
        lane = lax.broadcasted_iota(jnp.int32, (ROWS, 128), 1)
        docs = jnp.broadcast_to(seg[...], (ROWS, 128))
        line = lax.broadcasted_iota(jnp.int32, (ROWS, 128), 0)
        mine = jnp.where(line[0:ROPE, :] == docs[0:ROPE, :], 1.0, 0.0)
        kx[0:ROWS, :] = jnp.concatenate([lat[...].astype(F32), mine], axis=0).T.astype(BF16)
        in_slot = (line >= ROPE) & (line < ROPE + DOCS)
        q_mark = jnp.where(in_slot & (line - ROPE != docs), -BIG, 0.0).T
        pl.semaphore_wait(barrier, len(peers) + jnp.minimum(z, 2) + jnp.minimum(planes - 1 - z, 1))
        @pl.when(z >= 2)
        def _():
            pl.semaphore_signal(ready, inc=1, device_id=at((z + planes - 2) % planes, xh, c, y), device_id_type=MESH)

        def depart(k):
            send(("z", k), own_piece, piece(k, xh, y), at((z + k) % planes, xh, c, y), z + k < planes)

        def stage_z(k):
            arrive(("z", k), piece(k, xh, y), z >= k)

            @pl.when(z < k)
            def _():
                mark = lax.broadcasted_iota(jnp.int32, (QUARTER, 128), 1)
                mark = jnp.where((mark >= ROPE) & (mark < ROPE + DOCS), 1.0, 0.0)
                kx[pl.ds(start_of(k, c, xh, y), QUARTER), :] = jnp.concatenate(
                    [jnp.zeros((QUARTER, RANK), F32), mark], axis=1
                ).astype(BF16)

            mine = piece(k, xh, y)
            if k <= 2:
                send(
                    ("z", k + 2), mine, piece(k + 2, xh, y), at((z + 2) % planes, xh, c, y),
                    (z >= k) & (z + 2 < planes),
                )
            send(("x", k, 0), mine, mine, partner, xh == 1 if k == CHUNKS else None)
            for d in (1, 3, 2):
                send(("y", k, d), mine, mine, at(z, xh, c, (y + d) % 4))
            if ROUTES[k] == "S":
                for d in (1, 3, 2):
                    send(("x", k, d), mine, mine, at(z, 1 - xh, c, (y + d) % 4), xh == 1 if k == CHUNKS else None)

        def stage_x(k):
            far = xh == 0 if k == CHUNKS else None
            mine = piece(k, 1 - xh, y)
            arrive(("x", k, 0), mine, far)
            for d in (1, 3, 2):
                send(("y2", k, d), mine, mine, at(z, xh, c, (y + d) % 4), far)

        def stage_xs(k, d):
            mine = piece(k, xh, (y + 4 - d) % 4)
            arrive(("y", k, d), mine)
            send(("x", k, d), mine, mine, partner, xh == 1 if k == CHUNKS else None)

        def stage_ca(k):
            if ROUTES[k] != "X":
                for d in (1, 3, 2):
                    arrive(("y", k, d), piece(k, xh, (y + 4 - d) % 4))
            here = block(k, c, xh)
            send(("ca", k), here, here, twin, c == 1 if k == CHUNKS else None)

        def stage_cb(k):
            far = xh == 0 if k == CHUNKS else None
            if ROUTES[k] == "D":
                for d in (1, 3, 2):
                    arrive(("y2", k, d), piece(k, 1 - xh, (y + 4 - d) % 4), far)
            else:
                for d in range(4):
                    arrive(("x", k, d), piece(k, 1 - xh, (y + 4 - d) % 4 if d else y), far)
            here = block(k, c, 1 - xh)
            if k == CHUNKS:
                arrive("own", here, xh == 1)
            send(("cb", k), here, here, twin)

        def stage_done(k):
            arrive(("ca", k), block(k, 1 - c, xh))
            arrive(("cb", k), block(k, 1 - c, 1 - xh))

        def queries(p):
            base = 3 * 128 * p
            one = qv[:, base : base + 128]
            two = qv[:, base + 128 : base + 256].astype(F32)
            three = qv[:, base + 256 : base + 384].astype(F32)
            two_turned = pltpu.roll(two, 64, 1)
            three_turned = pltpu.roll(three, 64, 1)
            second = jnp.where(lane < 64, two_turned, three_turned).astype(BF16)
            for h, nope, pos in ((2 * p, one, two), (2 * p + 1, second, three_turned)):
                absorbed = lax.dot_general(
                    nope, wk[:, h * NOPE : (h + 1) * NOPE], NT, preferred_element_type=F32
                )
                qx[h * ROWS : (h + 1) * ROWS, 0:RANK] = (absorbed * FOLD).astype(BF16)
                qx[h * ROWS : (h + 1) * ROWS, RANK:WIDE] = jnp.where(lane < ROPE, pos * FOLD, q_mark).astype(BF16)

        def lane_max(scores):
            best = scores[:, 0:128]
            for i in range(1, scores.shape[1] // 128):
                best = jnp.maximum(best, scores[:, i * 128 : (i + 1) * 128])
            return best

        later = lax.broadcasted_iota(jnp.int32, (ROWS, ROWS), 1) > lax.broadcasted_iota(jnp.int32, (ROWS, ROWS), 0)
        causal = jnp.concatenate([jnp.where(later, -2.0 * BIG, 0.0)] * group, axis=0)

        def diagonal(g):
            r = slice(g * grow, (g + 1) * grow)
            scores = lax.dot_general(qx[r, :], kx[0:ROWS, :], NT, preferred_element_type=F32) + causal
            sc[r, 0:ROWS] = scores
            top[r, :] = scores

        def chunk_scores(k, g):
            r = slice(g * grow, (g + 1) * grow)
            first = ROWS + CHUNK * (k - 1)
            scores = lax.dot_general(qx[r, :], kx[first : first + CHUNK, :], NT, preferred_element_type=F32)
            sc[r, first : first + CHUNK] = scores
            top[r, :] = jnp.maximum(top[r, :], lane_max(scores))

        def lane_sum(weights):
            total = weights[:, 0:128]
            for i in range(1, weights.shape[1] // 128):
                total = total + weights[:, i * 128 : (i + 1) * 128]
            return total

        def finish(g):
            r = slice(g * grow, (g + 1) * grow)
            first = KEYS - CHUNK
            last = lax.dot_general(qx[r, :], kx[first:KEYS, :], NT, preferred_element_type=F32)
            high = jnp.max(jnp.maximum(top[r, :], lane_max(last)), axis=1, keepdims=True)
            early = jnp.exp2(sc[r, :] - high)
            late = jnp.exp2(last - high)
            total = jnp.sum(lane_sum(early) + lane_sum(late), axis=1, keepdims=True)
            mixed = jnp.dot(early.astype(BF16), kx[0:first, 0:RANK], preferred_element_type=F32)
            mixed = mixed + jnp.dot(late.astype(BF16), kx[first:KEYS, 0:RANK], preferred_element_type=F32)
            ob[r, :] = (mixed * (1.0 / total)).astype(BF16)
            for h in range(g * group, (g + 1) * group):
                att[:, h * VDIM : (h + 1) * VDIM] = jnp.dot(
                    ob[h * ROWS : (h + 1) * ROWS, :],
                    wv[:, h * VDIM : (h + 1) * VDIM],
                    preferred_element_type=F32,
                ).astype(BF16)
            mine = slice(g * group * VDIM, (g + 1) * group * VDIM)
            add = lax.dot_general(att[:, mine], wn[:, mine], NT, preferred_element_type=F32)
            if g == 0:
                proj[...] = add
            elif g < groups - 1:
                proj[...] += add
            else:
                total = proj[...] + add
                proj[...] = total
                part[...] = total.astype(BF16)

        depart(1)

        @pl.when(z + 2 < planes)
        def _():
            pl.semaphore_wait(ready, 1)

        when, first = sent.pop()
        pl.when(when)(first.wait_send)
        depart(2)
        send("own", own, block(CHUNKS, c, xh), partner, xh == 0)
        send(("ca", CHUNKS), own, block(CHUNKS, c, xh), twin, c == 0)
        loads[2].wait()
        loads[3].wait()
        steps = {
            "z": stage_z, "x": stage_x, "xs": stage_xs, "ca": stage_ca, "cb": stage_cb, "done": stage_done,
            "q": queries, "diag": diagonal, "qk": chunk_scores,
        }
        for step in PLAN:
            steps[step[0]](*step[1:])
        loads[4].wait()
        loads[5].wait()
        for g in range(groups):
            finish(g)
        store = pltpu.make_async_copy(att, att_hbm, ls.at[6])
        store.start()

        def sixteen(ref, yy, lower):
            return ref.at[pl.ds(pl.multiple_of(yy * QUARTER + lower * HALF, HALF), HALF)]

        for d in range(4):
            to = (y + d) % 4
            send(("rb", d), sixteen(part, to, 1), rsb.at[d], at(z, xh, c, to, 1 - s))
        for d in range(1, 4):
            to = (y + d) % 4
            send(("ra", d), sixteen(part, to, 0), rsa.at[d - 1], beside(to))

        def normal(total):
            low = total[:, 0:RANK]
            inverse = lax.rsqrt(jnp.sum(low * low, axis=1, keepdims=True) * (1.0 / RANK) + 1e-06)
            return (low * inverse).astype(BF16), total[:, RANK:LAT].astype(BF16)

        total = proj[pl.ds(pl.multiple_of(y * QUARTER, QUARTER), HALF), :]
        for d in range(1, 4):
            arrive(("ra", d), rsa.at[d - 1])
            total = total + rsa[d - 1].astype(F32)
        nla[:, 0:RANK], nla[:, RANK:LAT] = normal(total)
        for d in range(4):
            send(("na", d), nla, sixteen(nlb, y, 0), at(z, xh, c, (y + d) % 4, 1 - s))
        total = None
        for d in range(4):
            arrive(("rb", d), rsb.at[d])
            add = rsb[d].astype(F32)
            total = add if total is None else total + add
        lower = pl.ds(pl.multiple_of(y * QUARTER + HALF, HALF), HALF)
        nlb[lower, 0:RANK], nlb[lower, RANK:LAT] = normal(total)
        for d in range(1, 4):
            send(("nb", d), sixteen(nlb, y, 1), sixteen(nlb, y, 1), beside((y + d) % 4))
        for d in range(4):
            arrive(("na", d), sixteen(nlb, (y + 4 - d) % 4, 0))
        for d in range(1, 4):
            arrive(("nb", d), sixteen(nlb, (y + 4 - d) % 4, 1))
        out = pltpu.make_async_copy(nlb, next_hbm, ls.at[7])
        out.start()
        for when, one in sent:
            if when is None:
                one.wait_send()
            else:
                pl.when(when)(one.wait_send)
        store.wait()
        out.wait()

    def call(latent, queries, w_key, w_value, w_next, segments):
        return pl.pallas_call(
            kernel,
            out_shape=(
                jax.ShapeDtypeStruct((ROWS, heads * VDIM), BF16),
                jax.ShapeDtypeStruct((ROWS, LAT), BF16),
            ),
            in_specs=[pl.BlockSpec(memory_space=pl.ANY)] * 6,
            out_specs=[pl.BlockSpec(memory_space=pl.ANY)] * 2,
            scratch_shapes=[
                pltpu.VMEM((LAT, ROWS), BF16),
                pltpu.VMEM((1, ROWS), jnp.int32),
                pltpu.VMEM((ROWS, heads * (NOPE + ROPE)), BF16),
                pltpu.VMEM((RANK, heads * NOPE), BF16),
                pltpu.VMEM((RANK, heads * VDIM), BF16),
                pltpu.VMEM((LAT, heads * VDIM), BF16),
                pltpu.VMEM((rows_all, WIDE), BF16),
                pltpu.VMEM((KEYS, WIDE), BF16),
                pltpu.VMEM((rows_all, KEYS - CHUNK), F32),
                pltpu.VMEM((rows_all, 128), F32),
                pltpu.VMEM((rows_all, RANK), BF16),
                pltpu.VMEM((ROWS, heads * VDIM), BF16),
                pltpu.VMEM((ROWS, LAT), F32),
                pltpu.VMEM((ROWS, LAT), BF16),
                pltpu.VMEM((3, HALF, LAT), BF16),
                pltpu.VMEM((4, HALF, LAT), BF16),
                pltpu.VMEM((HALF, LAT), BF16),
                pltpu.VMEM((ROWS, LAT), BF16),
                pltpu.SemaphoreType.DMA((8,)),
                pltpu.SemaphoreType.DMA((SEMS,)),
                pltpu.SemaphoreType.DMA((SEMS,)),
                pltpu.SemaphoreType.REGULAR,
            ],
            compiler_params=pltpu.CompilerParams(
                collective_id=0, has_side_effects=True, vmem_limit_bytes=58 * 2**20
            ),
            name="attend",
        )(latent, queries, w_key, w_value, w_next, segments)

    return call


def hand_over(rows, turned, rows_out, turned_out):
    rows_out[0] = rows[...]
    turned_out[0] = turned[...].astype(F32).T.astype(BF16)


def results(rows, turned):
    return pl.pallas_call(
        hand_over,
        out_shape=(
            jax.ShapeDtypeStruct((1,) + rows.shape, BF16),
            jax.ShapeDtypeStruct((1, LAT, ROWS), BF16),
        ),
        name="results",
    )(rows, turned)


def solution(mesh):
    planes = mesh.shape["ctx"] // 4

    def local(latent, queries, w_key, w_value, w_next, segments):
        rows, mixed = make_kernel(planes, w_key.shape[2] // NOPE)(
            jnp.swapaxes(latent, 1, 2), queries, w_key, w_value, jnp.swapaxes(w_next, 1, 2), segments
        )
        attention, turned = results(rows, mixed)
        return attention, jnp.swapaxes(turned, 1, 2)

    in_specs = (
        P("section", "ctx", None),
        P("section", "ctx", "head"),
        P("section", None, "head"),
        P("section", None, "head"),
        P("section", "head", None),
        P("section", "ctx"),
    )
    out_specs = (P("section", "ctx", "head"), P("section", "ctx", None))
    return jax.shard_map(local, mesh=mesh, in_specs=in_specs, out_specs=out_specs, check_vma=False)
```

```python
import math

import jax
import jax.numpy as jnp
from jax import lax
from jax.experimental import pallas as pl
from jax.experimental.pallas import tpu as pltpu
from jax.sharding import PartitionSpec as P

MESH = pl.DeviceIdType.MESH
RANK = 512
ROPE = 64
NOPE = 128
VDIM = 128
LAT = 576
WIDE = 640
ROWS = 128
QUARTER = 32
SPLIT = 2
HALF = 16
CHUNK = 512
CHUNKS = 4
KEYS = ROWS + CHUNK * CHUNKS
DOCS = 4
BIG = float(2**30)
FOLD = math.log2(math.e) / math.sqrt(NOPE + ROPE)
NT = (((1,), (1,)), ((), ()))
F32 = jnp.float32
BF16 = jnp.bfloat16
SEMS = 72
ROUTES = ('', 'X', 'D', 'X', 'D')
PLAN = (
    ("q", 0), ("q", 1), ("q", 2), ("q", 3), ("q", 4), ("q", 5), ("q", 6), ("z", 1), ("q", 7), ("diag", 0),
    ("diag", 1), ("diag", 2), ("diag", 3), ("z", 2), ("xs", 1, 1), ("xs", 1, 3), ("xs", 1, 2), ("ca", 1),
    ("z", 3), ("x", 2), ("ca", 2), ("cb", 1), ("z", 4), ("xs", 3, 1), ("xs", 3, 3), ("done", 1), ("xs", 3, 2),
    ("ca", 3), ("qk", 1, 0), ("qk", 1, 1), ("qk", 1, 2), ("cb", 2), ("x", 4), ("qk", 1, 3), ("done", 2),
    ("qk", 2, 0), ("ca", 4), ("qk", 2, 1), ("qk", 2, 2), ("cb", 3), ("qk", 2, 3), ("early", 0), ("cb", 4),
    ("done", 3), ("early", 1), ("early", 2), ("early", 3), ("qk", 3, 0), ("qk", 3, 1), ("qk", 3, 2),
    ("qk", 3, 3), ("done", 4),
)


def make_kernel(planes, heads):
    rows_all = heads * ROWS
    group = 4
    grow = group * ROWS
    groups = heads // group
    ids = {}

    def kernel(lat_hbm, q_hbm, wk_hbm, wv_hbm, wn_hbm, seg_hbm, att_hbm, next_hbm,
               lat, seg, qv, wk, wv, wn, qx, kx, sc, top, late_top, sums, acc, ob, att, proj, part, rsa, rsb, nla, nlb,
               ls, ss, rs):
        s = lax.axis_index("section")
        t = lax.axis_index("ctx")
        y = lax.axis_index("head")
        z, xh, c = t // 4, (t // 2) % 2, t % 2

        def at(zz, xx, cc, yy, section=s):
            return {"section": section, "ctx": zz * 4 + xx * 2 + cc, "head": yy}

        right, left, across = (y + 1) % 4, (y + 3) % 4, (y + 2) % 4

        def load(i, src, dst):
            return pltpu.make_async_copy(src, dst, ls.at[i])

        loads = [
            load(0, lat_hbm.at[0], lat),
            load(1, seg_hbm, seg),
            load(2, q_hbm.at[0], qv),
            load(3, wk_hbm.at[0], wk),
            load(4, wv_hbm.at[0], wv),
            load(5, wn_hbm.at[0], wn),
        ]
        for one in loads:
            one.start()

        barrier = pltpu.get_barrier_semaphore()
        peers = [at(z, xh, 1 - c, y), at(z, 1 - xh, c, y)]
        peers += [at(z, xh, c, yy) for yy in (right, left, across)]
        peers += [at(z, xh, c, (y + d) % 4, 1 - s) for d in range(4)]
        for peer in peers:
            pl.semaphore_signal(barrier, inc=1, device_id=peer, device_id_type=MESH)
        @pl.when(z + 1 < planes)
        def _():
            pl.semaphore_signal(barrier, inc=1, device_id=at((z + 1) % planes, xh, c, y), device_id_type=MESH)

        @pl.when(z >= 1)
        def _():
            pl.semaphore_signal(barrier, inc=1, device_id=at((z + planes - 1) % planes, xh, c, y), device_id_type=MESH)

        def remote(name, src, dst, peer):
            i = ids.setdefault(name, len(ids))
            return pltpu.make_async_remote_copy(
                src_ref=src, dst_ref=dst, send_sem=ss.at[i], recv_sem=rs.at[i], device_id=peer, device_id_type=MESH
            )

        sent = []

        def send(name, src, dst, peer, when=None):
            one = remote(name, src, dst, peer)
            if when is None:
                one.start()
            else:
                pl.when(when)(one.start)
            sent.append((when, one))

        def arrive(name, dst, when=None):
            wait = remote(name, dst, dst, at(z, xh, c, right)).wait_recv
            if when is None:
                wait()
            else:
                pl.when(when)(wait)

        def start_of(k, cc, xx, yy=0):
            return pl.multiple_of(ROWS + CHUNK * (k - 1) + cc * 256 + xx * ROWS + yy * QUARTER, QUARTER)

        def block(k, cc, xx):
            return kx.at[pl.ds(start_of(k, cc, xx), ROWS)]

        def piece(k, xx, yy):
            return kx.at[pl.ds(start_of(k, c, xx, yy), QUARTER)]

        def beside(yy):
            return at(z, xh, c, yy)

        partner, twin = at(z, 1 - xh, c, y), at(z, xh, 1 - c, y)
        own = kx.at[pl.ds(0, ROWS)]
        own_piece = kx.at[pl.ds(pl.multiple_of(y * QUARTER, QUARTER), QUARTER)]

        loads[0].wait()
        loads[1].wait()
        lane = lax.broadcasted_iota(jnp.int32, (ROWS, 128), 1)
        docs = jnp.broadcast_to(seg[...], (ROWS, 128))
        line = lax.broadcasted_iota(jnp.int32, (ROWS, 128), 0)
        mine = jnp.where(line[0:ROPE, :] == docs[0:ROPE, :], 1.0, 0.0)
        kx[0:ROWS, :] = jnp.concatenate([lat[...].astype(F32), mine], axis=0).T.astype(BF16)
        in_slot = (line >= ROPE) & (line < ROPE + DOCS)
        q_mark = jnp.where(in_slot & (line - ROPE != docs), -BIG, 0.0).T
        pl.semaphore_wait(barrier, len(peers) + jnp.minimum(z, 1) + jnp.minimum(planes - 1 - z, 1))
        def stage_z(k):
            arrive(("z", k), piece(k, xh, y), z >= k)

            @pl.when(z < k)
            def _():
                mark = lax.broadcasted_iota(jnp.int32, (QUARTER, 128), 1)
                mark = jnp.where((mark >= ROPE) & (mark < ROPE + DOCS), 1.0, 0.0)
                kx[pl.ds(start_of(k, c, xh, y), QUARTER), :] = jnp.concatenate(
                    [jnp.zeros((QUARTER, RANK), F32), mark], axis=1
                ).astype(BF16)

            mine = piece(k, xh, y)
            if k < CHUNKS:
                send(
                    ("z", k + 1), mine, piece(k + 1, xh, y), at((z + 1) % planes, xh, c, y),
                    (z >= k) & (z + 1 < planes),
                )
            send(("x", k, 0), mine, mine, partner, xh == 1 if k == CHUNKS else None)
            for d in (1, 3, 2):
                send(("y", k, d), mine, mine, at(z, xh, c, (y + d) % 4))
            if ROUTES[k] == "S":
                for d in (1, 3, 2):
                    send(("x", k, d), mine, mine, at(z, 1 - xh, c, (y + d) % 4), xh == 1 if k == CHUNKS else None)

        def stage_x(k):
            far = xh == 0 if k == CHUNKS else None
            mine = piece(k, 1 - xh, y)
            arrive(("x", k, 0), mine, far)
            for d in (1, 3, 2):
                send(("y2", k, d), mine, mine, at(z, xh, c, (y + d) % 4), far)

        def stage_xs(k, d):
            mine = piece(k, xh, (y + 4 - d) % 4)
            arrive(("y", k, d), mine)
            send(("x", k, d), mine, mine, partner, xh == 1 if k == CHUNKS else None)

        def stage_ca(k):
            if ROUTES[k] != "X":
                for d in (1, 3, 2):
                    arrive(("y", k, d), piece(k, xh, (y + 4 - d) % 4))
            here = block(k, c, xh)
            send(("ca", k), here, here, twin, c == 1 if k == CHUNKS else None)

        def stage_cb(k):
            far = xh == 0 if k == CHUNKS else None
            if ROUTES[k] == "D":
                for d in (1, 3, 2):
                    arrive(("y2", k, d), piece(k, 1 - xh, (y + 4 - d) % 4), far)
            else:
                for d in range(4):
                    arrive(("x", k, d), piece(k, 1 - xh, (y + 4 - d) % 4 if d else y), far)
            here = block(k, c, 1 - xh)
            if k == CHUNKS:
                arrive("own", here, xh == 1)
            send(("cb", k), here, here, twin)

        def stage_done(k):
            arrive(("ca", k), block(k, 1 - c, xh))
            arrive(("cb", k), block(k, 1 - c, 1 - xh))

        def queries(p):
            base = 3 * 128 * p
            one = qv[:, base : base + 128]
            two = qv[:, base + 128 : base + 256].astype(F32)
            three = qv[:, base + 256 : base + 384].astype(F32)
            two_turned = pltpu.roll(two, 64, 1)
            three_turned = pltpu.roll(three, 64, 1)
            second = jnp.where(lane < 64, two_turned, three_turned).astype(BF16)
            for h, nope, pos in ((2 * p, one, two), (2 * p + 1, second, three_turned)):
                absorbed = lax.dot_general(
                    nope, wk[:, h * NOPE : (h + 1) * NOPE], NT, preferred_element_type=F32
                )
                qx[h * ROWS : (h + 1) * ROWS, 0:RANK] = (absorbed * FOLD).astype(BF16)
                qx[h * ROWS : (h + 1) * ROWS, RANK:WIDE] = jnp.where(lane < ROPE, pos * FOLD, q_mark).astype(BF16)

        def lane_max(scores):
            best = scores[:, 0:128]
            for i in range(1, scores.shape[1] // 128):
                best = jnp.maximum(best, scores[:, i * 128 : (i + 1) * 128])
            return best

        later = lax.broadcasted_iota(jnp.int32, (ROWS, ROWS), 1) > lax.broadcasted_iota(jnp.int32, (ROWS, ROWS), 0)
        causal = jnp.concatenate([jnp.where(later, -2.0 * BIG, 0.0)] * group, axis=0)

        def diagonal(g):
            r = slice(g * grow, (g + 1) * grow)
            scores = lax.dot_general(qx[r, :], kx[0:ROWS, :], NT, preferred_element_type=F32) + causal
            sc[r, 0:ROWS] = scores
            top[r, :] = scores

        def chunk_scores(k, g):
            r = slice(g * grow, (g + 1) * grow)
            first = ROWS + CHUNK * (k - 1)
            scores = lax.dot_general(qx[r, :], kx[first : first + CHUNK, :], NT, preferred_element_type=F32)
            sc[r, first : first + CHUNK] = scores
            best = lane_max(scores)
            if k <= SPLIT:
                top[r, :] = jnp.maximum(top[r, :], best)
            elif k == SPLIT + 1:
                late_top[r, :] = best
            else:
                late_top[r, :] = jnp.maximum(late_top[r, :], best)

        def lane_sum(weights):
            total = weights[:, 0:128]
            for i in range(1, weights.shape[1] // 128):
                total = total + weights[:, i * 128 : (i + 1) * 128]
            return total

        begin = ROWS + CHUNK * SPLIT

        def early(g):
            r = slice(g * grow, (g + 1) * grow)
            high = jnp.max(top[r, :], axis=1, keepdims=True)
            weights = jnp.exp2(sc[r, 0:begin] - high)
            sums[r, :] = lane_sum(weights)
            top[r, :] = jnp.broadcast_to(high, (grow, 128))
            acc[r, :] = jnp.dot(weights.astype(BF16), kx[0:begin, 0:RANK], preferred_element_type=F32)

        def finish(g):
            r = slice(g * grow, (g + 1) * grow)
            first = KEYS - CHUNK
            last = lax.dot_general(qx[r, :], kx[first:KEYS, :], NT, preferred_element_type=F32)
            best = lane_max(last)
            if SPLIT < CHUNKS - 1:
                best = jnp.maximum(best, late_top[r, :])
            high = jnp.max(jnp.maximum(best, top[r, :]), axis=1, keepdims=True)
            ratio = jnp.exp2(top[r, :] - high)
            late = jnp.exp2(last - high)
            total = sums[r, :] * ratio + lane_sum(late)
            mixed = acc[r, :] * jnp.concatenate([ratio] * (RANK // 128), axis=1)
            if SPLIT < CHUNKS - 1:
                middle = jnp.exp2(sc[r, begin:first] - high)
                total = total + lane_sum(middle)
                mixed = mixed + jnp.dot(middle.astype(BF16), kx[begin:first, 0:RANK], preferred_element_type=F32)
            mixed = mixed + jnp.dot(late.astype(BF16), kx[first:KEYS, 0:RANK], preferred_element_type=F32)
            total = jnp.sum(total, axis=1, keepdims=True)
            ob[r, :] = (mixed * (1.0 / total)).astype(BF16)
            for h in range(g * group, (g + 1) * group):
                att[:, h * VDIM : (h + 1) * VDIM] = jnp.dot(
                    ob[h * ROWS : (h + 1) * ROWS, :],
                    wv[:, h * VDIM : (h + 1) * VDIM],
                    preferred_element_type=F32,
                ).astype(BF16)
            mine = slice(g * group * VDIM, (g + 1) * group * VDIM)
            add = lax.dot_general(att[:, mine], wn[:, mine], NT, preferred_element_type=F32)
            if g == 0:
                proj[...] = add
            elif g < groups - 1:
                proj[...] += add
            else:
                total = proj[...] + add
                proj[...] = total
                part[...] = total.astype(BF16)

        send(("z", 1), own_piece, piece(1, xh, y), at((z + 1) % planes, xh, c, y), z + 1 < planes)
        send("own", own, block(CHUNKS, c, xh), partner, xh == 0)
        send(("ca", CHUNKS), own, block(CHUNKS, c, xh), twin, c == 0)
        loads[2].wait()
        loads[3].wait()
        steps = {
            "z": stage_z, "x": stage_x, "xs": stage_xs, "ca": stage_ca, "cb": stage_cb, "done": stage_done,
            "q": queries, "diag": diagonal, "qk": chunk_scores, "early": early,
        }
        for step in PLAN:
            steps[step[0]](*step[1:])
        loads[4].wait()
        loads[5].wait()
        for g in range(groups):
            finish(g)
        store = pltpu.make_async_copy(att, att_hbm, ls.at[6])
        store.start()

        def sixteen(ref, yy, lower):
            return ref.at[pl.ds(pl.multiple_of(yy * QUARTER + lower * HALF, HALF), HALF)]

        for d in range(4):
            to = (y + d) % 4
            send(("rb", d), sixteen(part, to, 1), rsb.at[d], at(z, xh, c, to, 1 - s))
        for d in range(1, 4):
            to = (y + d) % 4
            send(("ra", d), sixteen(part, to, 0), rsa.at[d - 1], beside(to))

        def normal(total):
            low = total[:, 0:RANK]
            inverse = lax.rsqrt(jnp.sum(low * low, axis=1, keepdims=True) * (1.0 / RANK) + 1e-06)
            return (low * inverse).astype(BF16), total[:, RANK:LAT].astype(BF16)

        total = proj[pl.ds(pl.multiple_of(y * QUARTER, QUARTER), HALF), :]
        for d in range(1, 4):
            arrive(("ra", d), rsa.at[d - 1])
            total = total + rsa[d - 1].astype(F32)
        nla[:, 0:RANK], nla[:, RANK:LAT] = normal(total)
        for d in range(4):
            send(("na", d), nla, sixteen(nlb, y, 0), at(z, xh, c, (y + d) % 4, 1 - s))
        total = None
        for d in range(4):
            arrive(("rb", d), rsb.at[d])
            add = rsb[d].astype(F32)
            total = add if total is None else total + add
        lower = pl.ds(pl.multiple_of(y * QUARTER + HALF, HALF), HALF)
        nlb[lower, 0:RANK], nlb[lower, RANK:LAT] = normal(total)
        for d in range(1, 4):
            send(("nb", d), sixteen(nlb, y, 1), sixteen(nlb, y, 1), beside((y + d) % 4))
        for d in range(4):
            arrive(("na", d), sixteen(nlb, (y + 4 - d) % 4, 0))
        for d in range(1, 4):
            arrive(("nb", d), sixteen(nlb, (y + 4 - d) % 4, 1))
        out = pltpu.make_async_copy(nlb, next_hbm, ls.at[7])
        out.start()
        for when, one in sent:
            if when is None:
                one.wait_send()
            else:
                pl.when(when)(one.wait_send)
        store.wait()
        out.wait()

    def call(latent, queries, w_key, w_value, w_next, segments):
        return pl.pallas_call(
            kernel,
            out_shape=(
                jax.ShapeDtypeStruct((ROWS, heads * VDIM), BF16),
                jax.ShapeDtypeStruct((ROWS, LAT), BF16),
            ),
            in_specs=[pl.BlockSpec(memory_space=pl.ANY)] * 6,
            out_specs=[pl.BlockSpec(memory_space=pl.ANY)] * 2,
            scratch_shapes=[
                pltpu.VMEM((LAT, ROWS), BF16),
                pltpu.VMEM((1, ROWS), jnp.int32),
                pltpu.VMEM((ROWS, heads * (NOPE + ROPE)), BF16),
                pltpu.VMEM((RANK, heads * NOPE), BF16),
                pltpu.VMEM((RANK, heads * VDIM), BF16),
                pltpu.VMEM((LAT, heads * VDIM), BF16),
                pltpu.VMEM((rows_all, WIDE), BF16),
                pltpu.VMEM((KEYS, WIDE), BF16),
                pltpu.VMEM((rows_all, KEYS - CHUNK), F32),
                pltpu.VMEM((rows_all, 128), F32),
                pltpu.VMEM((rows_all, 128), F32),
                pltpu.VMEM((rows_all, 128), F32),
                pltpu.VMEM((rows_all, RANK), F32),
                pltpu.VMEM((rows_all, RANK), BF16),
                pltpu.VMEM((ROWS, heads * VDIM), BF16),
                pltpu.VMEM((ROWS, LAT), F32),
                pltpu.VMEM((ROWS, LAT), BF16),
                pltpu.VMEM((3, HALF, LAT), BF16),
                pltpu.VMEM((4, HALF, LAT), BF16),
                pltpu.VMEM((HALF, LAT), BF16),
                pltpu.VMEM((ROWS, LAT), BF16),
                pltpu.SemaphoreType.DMA((8,)),
                pltpu.SemaphoreType.DMA((SEMS,)),
                pltpu.SemaphoreType.DMA((SEMS,)),
            ],
            compiler_params=pltpu.CompilerParams(
                collective_id=0, has_side_effects=True, vmem_limit_bytes=58 * 2**20
            ),
            name="attend",
        )(latent, queries, w_key, w_value, w_next, segments)

    return call


def hand_over(rows, turned, rows_out, turned_out):
    rows_out[0] = rows[...]
    turned_out[0] = turned[...].astype(F32).T.astype(BF16)


def results(rows, turned):
    return pl.pallas_call(
        hand_over,
        out_shape=(
            jax.ShapeDtypeStruct((1,) + rows.shape, BF16),
            jax.ShapeDtypeStruct((1, LAT, ROWS), BF16),
        ),
        name="results",
    )(rows, turned)


def solution(mesh):
    planes = mesh.shape["ctx"] // 4

    def local(latent, queries, w_key, w_value, w_next, segments):
        rows, mixed = make_kernel(planes, w_key.shape[2] // NOPE)(
            jnp.swapaxes(latent, 1, 2), queries, w_key, w_value, jnp.swapaxes(w_next, 1, 2), segments
        )
        attention, turned = results(rows, mixed)
        return attention, jnp.swapaxes(turned, 1, 2)

    in_specs = (
        P("section", "ctx", None),
        P("section", "ctx", "head"),
        P("section", None, "head"),
        P("section", None, "head"),
        P("section", "head", None),
        P("section", "ctx"),
    )
    out_specs = (P("section", "ctx", "head"), P("section", "ctx", None))
    return jax.shard_map(local, mesh=mesh, in_specs=in_specs, out_specs=out_specs, check_vma=False)
```

```python
import math

import jax
import jax.numpy as jnp
from jax import lax
from jax.experimental import pallas as pl
from jax.experimental.pallas import tpu as pltpu
from jax.sharding import PartitionSpec as P

MESH = pl.DeviceIdType.MESH
RANK = 512
ROPE = 64
NOPE = 128
VDIM = 128
LAT = 576
WIDE = 640
ROWS = 128
QUARTER = 32
SPLIT = 2
HALF = 16
CHUNK = 512
CHUNKS = 4
KEYS = ROWS + CHUNK * CHUNKS
DOCS = 4
BIG = float(2**30)
FOLD = math.log2(math.e) / math.sqrt(NOPE + ROPE)
NT = (((1,), (1,)), ((), ()))
F32 = jnp.float32
BF16 = jnp.bfloat16
SEMS = 72
ROUTES = ('', 'X', 'D', 'X', 'D')
PLAN = (
    ("q", 0), ("q", 1), ("q", 2), ("q", 3), ("q", 4), ("q", 5), ("q", 6), ("z", 1), ("q", 7), ("diag", 0),
    ("diag", 1), ("diag", 2), ("diag", 3), ("z", 2), ("xs", 1, 1), ("xs", 1, 3), ("xs", 1, 2), ("ca", 1),
    ("z", 3), ("x", 2), ("ca", 2), ("cb", 1), ("z", 4), ("xs", 3, 1), ("xs", 3, 3), ("done", 1), ("xs", 3, 2),
    ("ca", 3), ("qk", 1, 0), ("qk", 1, 1), ("qk", 1, 2), ("cb", 2), ("x", 4), ("qk", 1, 3), ("done", 2),
    ("qk", 2, 0), ("ca", 4), ("qk", 2, 1), ("qk", 2, 2), ("cb", 3), ("qk", 2, 3), ("early", 0), ("early", 1),
    ("early", 2), ("early", 3), ("cb", 4), ("done", 3), ("qk", 3, 0), ("qk", 3, 1), ("qk", 3, 2),
    ("qk", 3, 3), ("done", 4),
)


def make_kernel(planes, heads):
    rows_all = heads * ROWS
    group = 4
    grow = group * ROWS
    groups = heads // group
    ids = {}

    def kernel(lat_hbm, q_hbm, wk_hbm, wv_hbm, wn_hbm, seg_hbm, att_hbm, next_hbm,
               lat, seg, qv, wk, wv, wn, qx, kx, sc, top, late_top, sums, acc, ob, att, proj, part, rsa, rsb, nla, nlb,
               ls, ss, rs):
        s = lax.axis_index("section")
        t = lax.axis_index("ctx")
        y = lax.axis_index("head")
        z, xh, c = t // 4, (t // 2) % 2, t % 2

        def at(zz, xx, cc, yy, section=s):
            return {"section": section, "ctx": zz * 4 + xx * 2 + cc, "head": yy}

        right, left, across = (y + 1) % 4, (y + 3) % 4, (y + 2) % 4

        def load(i, src, dst):
            return pltpu.make_async_copy(src, dst, ls.at[i])

        loads = [
            load(0, lat_hbm.at[0], lat),
            load(1, seg_hbm, seg),
            load(2, q_hbm.at[0], qv),
            load(3, wk_hbm.at[0], wk),
            load(4, wv_hbm.at[0], wv),
            load(5, wn_hbm.at[0], wn),
        ]
        for one in loads:
            one.start()

        barrier = pltpu.get_barrier_semaphore()
        peers = [at(z, xh, 1 - c, y), at(z, 1 - xh, c, y)]
        peers += [at(z, xh, c, yy) for yy in (right, left, across)]
        peers += [at(z, xh, c, (y + d) % 4, 1 - s) for d in range(4)]
        for peer in peers:
            pl.semaphore_signal(barrier, inc=1, device_id=peer, device_id_type=MESH)
        @pl.when(z + 1 < planes)
        def _():
            pl.semaphore_signal(barrier, inc=1, device_id=at((z + 1) % planes, xh, c, y), device_id_type=MESH)

        @pl.when(z >= 1)
        def _():
            pl.semaphore_signal(barrier, inc=1, device_id=at((z + planes - 1) % planes, xh, c, y), device_id_type=MESH)

        def remote(name, src, dst, peer):
            i = ids.setdefault(name, len(ids))
            return pltpu.make_async_remote_copy(
                src_ref=src, dst_ref=dst, send_sem=ss.at[i], recv_sem=rs.at[i], device_id=peer, device_id_type=MESH
            )

        sent = []

        def send(name, src, dst, peer, when=None):
            one = remote(name, src, dst, peer)
            if when is None:
                one.start()
            else:
                pl.when(when)(one.start)
            sent.append((when, one))

        def arrive(name, dst, when=None):
            wait = remote(name, dst, dst, at(z, xh, c, right)).wait_recv
            if when is None:
                wait()
            else:
                pl.when(when)(wait)

        def start_of(k, cc, xx, yy=0):
            return pl.multiple_of(ROWS + CHUNK * (k - 1) + cc * 256 + xx * ROWS + yy * QUARTER, QUARTER)

        def block(k, cc, xx):
            return kx.at[pl.ds(start_of(k, cc, xx), ROWS)]

        def piece(k, xx, yy):
            return kx.at[pl.ds(start_of(k, c, xx, yy), QUARTER)]

        def beside(yy):
            return at(z, xh, c, yy)

        partner, twin = at(z, 1 - xh, c, y), at(z, xh, 1 - c, y)
        own = kx.at[pl.ds(0, ROWS)]
        own_piece = kx.at[pl.ds(pl.multiple_of(y * QUARTER, QUARTER), QUARTER)]

        loads[0].wait()
        loads[1].wait()
        lane = lax.broadcasted_iota(jnp.int32, (ROWS, 128), 1)
        docs = jnp.broadcast_to(seg[...], (ROWS, 128))
        line = lax.broadcasted_iota(jnp.int32, (ROWS, 128), 0)
        mine = jnp.where(line[0:ROPE, :] == docs[0:ROPE, :], 1.0, 0.0)
        kx[0:ROWS, :] = jnp.concatenate([lat[...].astype(F32), mine], axis=0).T.astype(BF16)
        in_slot = (line >= ROPE) & (line < ROPE + DOCS)
        q_mark = jnp.where(in_slot & (line - ROPE != docs), -BIG, 0.0).T
        pl.semaphore_wait(barrier, len(peers) + jnp.minimum(z, 1) + jnp.minimum(planes - 1 - z, 1))
        def stage_z(k):
            arrive(("z", k), piece(k, xh, y), z >= k)

            @pl.when(z < k)
            def _():
                mark = lax.broadcasted_iota(jnp.int32, (QUARTER, 128), 1)
                mark = jnp.where((mark >= ROPE) & (mark < ROPE + DOCS), 1.0, 0.0)
                kx[pl.ds(start_of(k, c, xh, y), QUARTER), :] = jnp.concatenate(
                    [jnp.zeros((QUARTER, RANK), F32), mark], axis=1
                ).astype(BF16)

            mine = piece(k, xh, y)
            if k < CHUNKS:
                send(
                    ("z", k + 1), mine, piece(k + 1, xh, y), at((z + 1) % planes, xh, c, y),
                    (z >= k) & (z + 1 < planes),
                )
            send(("x", k, 0), mine, mine, partner, xh == 1 if k == CHUNKS else None)
            for d in (1, 3, 2):
                send(("y", k, d), mine, mine, at(z, xh, c, (y + d) % 4))
            if ROUTES[k] == "S":
                for d in (1, 3, 2):
                    send(("x", k, d), mine, mine, at(z, 1 - xh, c, (y + d) % 4), xh == 1 if k == CHUNKS else None)

        def stage_x(k):
            far = xh == 0 if k == CHUNKS else None
            mine = piece(k, 1 - xh, y)
            arrive(("x", k, 0), mine, far)
            for d in (1, 3, 2):
                send(("y2", k, d), mine, mine, at(z, xh, c, (y + d) % 4), far)

        def stage_xs(k, d):
            mine = piece(k, xh, (y + 4 - d) % 4)
            arrive(("y", k, d), mine)
            send(("x", k, d), mine, mine, partner, xh == 1 if k == CHUNKS else None)

        def stage_ca(k):
            if ROUTES[k] != "X":
                for d in (1, 3, 2):
                    arrive(("y", k, d), piece(k, xh, (y + 4 - d) % 4))
            here = block(k, c, xh)
            send(("ca", k), here, here, twin, c == 1 if k == CHUNKS else None)

        def stage_cb(k):
            far = xh == 0 if k == CHUNKS else None
            if ROUTES[k] == "D":
                for d in (1, 3, 2):
                    arrive(("y2", k, d), piece(k, 1 - xh, (y + 4 - d) % 4), far)
            else:
                for d in range(4):
                    arrive(("x", k, d), piece(k, 1 - xh, (y + 4 - d) % 4 if d else y), far)
            here = block(k, c, 1 - xh)
            if k == CHUNKS:
                arrive("own", here, xh == 1)
            send(("cb", k), here, here, twin)

        def stage_done(k):
            arrive(("ca", k), block(k, 1 - c, xh))
            arrive(("cb", k), block(k, 1 - c, 1 - xh))

        def queries(p):
            base = 3 * 128 * p
            one = qv[:, base : base + 128]
            two = qv[:, base + 128 : base + 256].astype(F32)
            three = qv[:, base + 256 : base + 384].astype(F32)
            two_turned = pltpu.roll(two, 64, 1)
            three_turned = pltpu.roll(three, 64, 1)
            second = jnp.where(lane < 64, two_turned, three_turned).astype(BF16)
            for h, nope, pos in ((2 * p, one, two), (2 * p + 1, second, three_turned)):
                absorbed = lax.dot_general(
                    nope, wk[:, h * NOPE : (h + 1) * NOPE], NT, preferred_element_type=F32
                )
                qx[h * ROWS : (h + 1) * ROWS, 0:RANK] = (absorbed * FOLD).astype(BF16)
                qx[h * ROWS : (h + 1) * ROWS, RANK:WIDE] = jnp.where(lane < ROPE, pos * FOLD, q_mark).astype(BF16)

        def lane_max(scores):
            best = scores[:, 0:128]
            for i in range(1, scores.shape[1] // 128):
                best = jnp.maximum(best, scores[:, i * 128 : (i + 1) * 128])
            return best

        later = lax.broadcasted_iota(jnp.int32, (ROWS, ROWS), 1) > lax.broadcasted_iota(jnp.int32, (ROWS, ROWS), 0)
        causal = jnp.concatenate([jnp.where(later, -2.0 * BIG, 0.0)] * group, axis=0)

        def diagonal(g):
            r = slice(g * grow, (g + 1) * grow)
            scores = lax.dot_general(qx[r, :], kx[0:ROWS, :], NT, preferred_element_type=F32) + causal
            sc[r, 0:ROWS] = scores
            top[r, :] = scores

        def chunk_scores(k, g):
            r = slice(g * grow, (g + 1) * grow)
            first = ROWS + CHUNK * (k - 1)
            scores = lax.dot_general(qx[r, :], kx[first : first + CHUNK, :], NT, preferred_element_type=F32)
            sc[r, first : first + CHUNK] = scores
            best = lane_max(scores)
            if k <= SPLIT:
                top[r, :] = jnp.maximum(top[r, :], best)
            elif k == SPLIT + 1:
                late_top[r, :] = best
            else:
                late_top[r, :] = jnp.maximum(late_top[r, :], best)

        def lane_sum(weights):
            total = weights[:, 0:128]
            for i in range(1, weights.shape[1] // 128):
                total = total + weights[:, i * 128 : (i + 1) * 128]
            return total

        begin = ROWS + CHUNK * SPLIT

        def early(g):
            r = slice(g * grow, (g + 1) * grow)
            high = jnp.max(top[r, :], axis=1, keepdims=True)
            weights = jnp.exp2(sc[r, 0:begin] - high)
            sums[r, :] = lane_sum(weights)
            top[r, :] = jnp.broadcast_to(high, (grow, 128))
            acc[r, :] = jnp.dot(weights.astype(BF16), kx[0:begin, 0:RANK], preferred_element_type=F32)

        def finish(g):
            r = slice(g * grow, (g + 1) * grow)
            first = KEYS - CHUNK
            last = lax.dot_general(qx[r, :], kx[first:KEYS, :], NT, preferred_element_type=F32)
            best = lane_max(last)
            if SPLIT < CHUNKS - 1:
                best = jnp.maximum(best, late_top[r, :])
            high = jnp.max(jnp.maximum(best, top[r, :]), axis=1, keepdims=True)
            ratio = jnp.exp2(top[r, :] - high)
            late = jnp.exp2(last - high)
            total = sums[r, :] * ratio + lane_sum(late)
            mixed = acc[r, :] * jnp.concatenate([ratio] * (RANK // 128), axis=1)
            if SPLIT < CHUNKS - 1:
                middle = jnp.exp2(sc[r, begin:first] - high)
                total = total + lane_sum(middle)
                mixed = mixed + jnp.dot(middle.astype(BF16), kx[begin:first, 0:RANK], preferred_element_type=F32)
            mixed = mixed + jnp.dot(late.astype(BF16), kx[first:KEYS, 0:RANK], preferred_element_type=F32)
            total = jnp.sum(total, axis=1, keepdims=True)
            ob[r, :] = (mixed * (1.0 / total)).astype(BF16)
            for h in range(g * group, (g + 1) * group):
                att[:, h * VDIM : (h + 1) * VDIM] = jnp.dot(
                    ob[h * ROWS : (h + 1) * ROWS, :],
                    wv[:, h * VDIM : (h + 1) * VDIM],
                    preferred_element_type=F32,
                ).astype(BF16)
            mine = slice(g * group * VDIM, (g + 1) * group * VDIM)
            add = lax.dot_general(att[:, mine], wn[:, mine], NT, preferred_element_type=F32)
            if g == 0:
                proj[...] = add
            elif g < groups - 1:
                proj[...] += add
            else:
                total = proj[...] + add
                proj[...] = total
                part[...] = total.astype(BF16)

        send(("z", 1), own_piece, piece(1, xh, y), at((z + 1) % planes, xh, c, y), z + 1 < planes)
        send("own", own, block(CHUNKS, c, xh), partner, xh == 0)
        send(("ca", CHUNKS), own, block(CHUNKS, c, xh), twin, c == 0)
        loads[2].wait()
        loads[3].wait()
        steps = {
            "z": stage_z, "x": stage_x, "xs": stage_xs, "ca": stage_ca, "cb": stage_cb, "done": stage_done,
            "q": queries, "diag": diagonal, "qk": chunk_scores, "early": early,
        }
        for step in PLAN:
            steps[step[0]](*step[1:])
        loads[4].wait()
        loads[5].wait()
        for g in range(groups):
            finish(g)
        store = pltpu.make_async_copy(att, att_hbm, ls.at[6])
        store.start()

        def sixteen(ref, yy, lower):
            return ref.at[pl.ds(pl.multiple_of(yy * QUARTER + lower * HALF, HALF), HALF)]

        for d in range(4):
            to = (y + d) % 4
            send(("rb", d), sixteen(part, to, 1), rsb.at[d], at(z, xh, c, to, 1 - s))
        for d in range(1, 4):
            to = (y + d) % 4
            send(("ra", d), sixteen(part, to, 0), rsa.at[d - 1], beside(to))

        def normal(total):
            low = total[:, 0:RANK]
            inverse = lax.rsqrt(jnp.sum(low * low, axis=1, keepdims=True) * (1.0 / RANK) + 1e-06)
            return (low * inverse).astype(BF16), total[:, RANK:LAT].astype(BF16)

        total = proj[pl.ds(pl.multiple_of(y * QUARTER, QUARTER), HALF), :]
        for d in range(1, 4):
            arrive(("ra", d), rsa.at[d - 1])
            total = total + rsa[d - 1].astype(F32)
        nla[:, 0:RANK], nla[:, RANK:LAT] = normal(total)
        for d in range(4):
            send(("na", d), nla, sixteen(nlb, y, 0), at(z, xh, c, (y + d) % 4, 1 - s))
        total = None
        for d in range(4):
            arrive(("rb", d), rsb.at[d])
            add = rsb[d].astype(F32)
            total = add if total is None else total + add
        lower = pl.ds(pl.multiple_of(y * QUARTER + HALF, HALF), HALF)
        nlb[lower, 0:RANK], nlb[lower, RANK:LAT] = normal(total)
        for d in range(1, 4):
            send(("nb", d), sixteen(nlb, y, 1), sixteen(nlb, y, 1), beside((y + d) % 4))
        for d in range(4):
            arrive(("na", d), sixteen(nlb, (y + 4 - d) % 4, 0))
        for d in range(1, 4):
            arrive(("nb", d), sixteen(nlb, (y + 4 - d) % 4, 1))
        out = pltpu.make_async_copy(nlb, next_hbm, ls.at[7])
        out.start()
        for when, one in sent:
            if when is None:
                one.wait_send()
            else:
                pl.when(when)(one.wait_send)
        store.wait()
        out.wait()

    def call(latent, queries, w_key, w_value, w_next, segments):
        return pl.pallas_call(
            kernel,
            out_shape=(
                jax.ShapeDtypeStruct((ROWS, heads * VDIM), BF16),
                jax.ShapeDtypeStruct((ROWS, LAT), BF16),
            ),
            in_specs=[pl.BlockSpec(memory_space=pl.ANY)] * 6,
            out_specs=[pl.BlockSpec(memory_space=pl.ANY)] * 2,
            scratch_shapes=[
                pltpu.VMEM((LAT, ROWS), BF16),
                pltpu.VMEM((1, ROWS), jnp.int32),
                pltpu.VMEM((ROWS, heads * (NOPE + ROPE)), BF16),
                pltpu.VMEM((RANK, heads * NOPE), BF16),
                pltpu.VMEM((RANK, heads * VDIM), BF16),
                pltpu.VMEM((LAT, heads * VDIM), BF16),
                pltpu.VMEM((rows_all, WIDE), BF16),
                pltpu.VMEM((KEYS, WIDE), BF16),
                pltpu.VMEM((rows_all, KEYS - CHUNK), F32),
                pltpu.VMEM((rows_all, 128), F32),
                pltpu.VMEM((rows_all, 128), F32),
                pltpu.VMEM((rows_all, 128), F32),
                pltpu.VMEM((rows_all, RANK), F32),
                pltpu.VMEM((rows_all, RANK), BF16),
                pltpu.VMEM((ROWS, heads * VDIM), BF16),
                pltpu.VMEM((ROWS, LAT), F32),
                pltpu.VMEM((ROWS, LAT), BF16),
                pltpu.VMEM((3, HALF, LAT), BF16),
                pltpu.VMEM((4, HALF, LAT), BF16),
                pltpu.VMEM((HALF, LAT), BF16),
                pltpu.VMEM((ROWS, LAT), BF16),
                pltpu.SemaphoreType.DMA((8,)),
                pltpu.SemaphoreType.DMA((SEMS,)),
                pltpu.SemaphoreType.DMA((SEMS,)),
            ],
            compiler_params=pltpu.CompilerParams(
                collective_id=0, has_side_effects=True, vmem_limit_bytes=58 * 2**20
            ),
            name="attend",
        )(latent, queries, w_key, w_value, w_next, segments)

    return call


def hand_over(rows, turned, rows_out, turned_out):
    rows_out[0] = rows[...]
    turned_out[0] = turned[...].astype(F32).T.astype(BF16)


def results(rows, turned):
    return pl.pallas_call(
        hand_over,
        out_shape=(
            jax.ShapeDtypeStruct((1,) + rows.shape, BF16),
            jax.ShapeDtypeStruct((1, LAT, ROWS), BF16),
        ),
        name="results",
    )(rows, turned)


def solution(mesh):
    planes = mesh.shape["ctx"] // 4

    def local(latent, queries, w_key, w_value, w_next, segments):
        rows, mixed = make_kernel(planes, w_key.shape[2] // NOPE)(
            jnp.swapaxes(latent, 1, 2), queries, w_key, w_value, jnp.swapaxes(w_next, 1, 2), segments
        )
        attention, turned = results(rows, mixed)
        return attention, jnp.swapaxes(turned, 1, 2)

    in_specs = (
        P("section", "ctx", None),
        P("section", "ctx", "head"),
        P("section", None, "head"),
        P("section", None, "head"),
        P("section", "head", None),
        P("section", "ctx"),
    )
    out_specs = (P("section", "ctx", "head"), P("section", "ctx", None))
    return jax.shard_map(local, mesh=mesh, in_specs=in_specs, out_specs=out_specs, check_vma=False)
```

```python
import math

import jax
import jax.numpy as jnp
from jax import lax
from jax.experimental import pallas as pl
from jax.experimental.pallas import tpu as pltpu
from jax.sharding import PartitionSpec as P

MESH = pl.DeviceIdType.MESH
RANK = 512
ROPE = 64
NOPE = 128
VDIM = 128
LAT = 576
WIDE = 640
ROWS = 128
QUARTER = 32
SPLIT = 2
HALF = 16
CHUNK = 512
CHUNKS = 4
KEYS = ROWS + CHUNK * CHUNKS
DOCS = 4
BIG = float(2**30)
FOLD = math.log2(math.e) / math.sqrt(NOPE + ROPE)
NT = (((1,), (1,)), ((), ()))
F32 = jnp.float32
BF16 = jnp.bfloat16
SEMS = 72
ROUTES = ('', 'X', 'D', 'X', 'D')
PLAN = (
    ("q", 0), ("q", 1), ("q", 2), ("q", 3), ("q", 4), ("q", 5), ("q", 6), ("z", 1), ("q", 7), ("diag", 0),
    ("diag", 1), ("diag", 2), ("diag", 3), ("z", 2), ("xs", 1, 1), ("xs", 1, 3), ("xs", 1, 2), ("ca", 1),
    ("z", 3), ("x", 2), ("ca", 2), ("cb", 1), ("z", 4), ("xs", 3, 1), ("xs", 3, 3), ("done", 1), ("xs", 3, 2),
    ("ca", 3), ("qk", 1, 0), ("qk", 1, 1), ("qk", 1, 2), ("cb", 2), ("x", 4), ("qk", 1, 3), ("done", 2),
    ("qk", 2, 0), ("ca", 4), ("qk", 2, 1), ("qk", 2, 2), ("cb", 3), ("qk", 2, 3), ("early", 0), ("early", 1),
    ("early", 2), ("early", 3), ("cb", 4), ("done", 3), ("qk", 3, 0), ("qk", 3, 1), ("qk", 3, 2),
    ("qk", 3, 3), ("done", 4),
)


def make_kernel(planes, heads):
    rows_all = heads * ROWS
    group = 4
    grow = group * ROWS
    groups = heads // group
    ids = {}

    def kernel(lat_hbm, q_hbm, wk_hbm, wv_hbm, wn_hbm, seg_hbm, att_hbm, next_hbm,
               lat, seg, qv, wk, wv, wn, qx, kx, sc, top, late_top, sums, acc, ob, att, proj, part, rsa, rsb, nla, nlb,
               ls, ss, rs):
        s = lax.axis_index("section")
        t = lax.axis_index("ctx")
        y = lax.axis_index("head")
        z, xh, c = t // 4, (t // 2) % 2, t % 2

        def at(zz, xx, cc, yy, section=s):
            return {"section": section, "ctx": zz * 4 + xx * 2 + cc, "head": yy}

        right, left, across = (y + 1) % 4, (y + 3) % 4, (y + 2) % 4

        def load(i, src, dst):
            return pltpu.make_async_copy(src, dst, ls.at[i])

        loads = [
            load(0, lat_hbm.at[0], lat),
            load(1, seg_hbm, seg),
            load(2, q_hbm.at[0], qv),
            load(3, wk_hbm.at[0], wk),
            load(4, wv_hbm.at[0], wv),
            load(5, wn_hbm.at[0], wn),
        ]
        for one in loads:
            one.start()

        barrier = pltpu.get_barrier_semaphore()
        peers = [at(z, xh, 1 - c, y), at(z, 1 - xh, c, y)]
        peers += [at(z, xh, c, yy) for yy in (right, left, across)]
        peers += [at(z, xh, c, (y + d) % 4, 1 - s) for d in range(4)]
        for peer in peers:
            pl.semaphore_signal(barrier, inc=1, device_id=peer, device_id_type=MESH)
        @pl.when(z + 1 < planes)
        def _():
            pl.semaphore_signal(barrier, inc=1, device_id=at((z + 1) % planes, xh, c, y), device_id_type=MESH)

        @pl.when(z >= 1)
        def _():
            pl.semaphore_signal(barrier, inc=1, device_id=at((z + planes - 1) % planes, xh, c, y), device_id_type=MESH)

        def remote(name, src, dst, peer):
            i = ids.setdefault(name, len(ids))
            return pltpu.make_async_remote_copy(
                src_ref=src, dst_ref=dst, send_sem=ss.at[i], recv_sem=rs.at[i], device_id=peer, device_id_type=MESH
            )

        sent = []

        def send(name, src, dst, peer, when=None):
            one = remote(name, src, dst, peer)
            if when is None:
                one.start()
            else:
                pl.when(when)(one.start)
            sent.append((when, one))

        def arrive(name, dst, when=None):
            wait = remote(name, dst, dst, at(z, xh, c, right)).wait_recv
            if when is None:
                wait()
            else:
                pl.when(when)(wait)

        def start_of(k, cc, xx, yy=0):
            return pl.multiple_of(ROWS + CHUNK * (k - 1) + cc * 256 + xx * ROWS + yy * QUARTER, QUARTER)

        def block(k, cc, xx):
            return kx.at[pl.ds(start_of(k, cc, xx), ROWS)]

        def piece(k, xx, yy):
            return kx.at[pl.ds(start_of(k, c, xx, yy), QUARTER)]

        def beside(yy):
            return at(z, xh, c, yy)

        partner, twin = at(z, 1 - xh, c, y), at(z, xh, 1 - c, y)
        own = kx.at[pl.ds(0, ROWS)]
        own_piece = kx.at[pl.ds(pl.multiple_of(y * QUARTER, QUARTER), QUARTER)]

        loads[0].wait()
        loads[1].wait()
        lane = lax.broadcasted_iota(jnp.int32, (ROWS, 128), 1)
        docs = jnp.broadcast_to(seg[...], (ROWS, 128))
        line = lax.broadcasted_iota(jnp.int32, (ROWS, 128), 0)
        mine = jnp.where(line[0:ROPE, :] == docs[0:ROPE, :], 1.0, 0.0)
        kx[0:ROWS, :] = jnp.concatenate([lat[...].astype(F32), mine], axis=0).T.astype(BF16)
        in_slot = (line >= ROPE) & (line < ROPE + DOCS)
        q_mark = jnp.where(in_slot & (line - ROPE != docs), -BIG, 0.0).T
        pl.semaphore_wait(barrier, len(peers) + jnp.minimum(z, 1) + jnp.minimum(planes - 1 - z, 1))
        def stage_z(k):
            arrive(("z", k), piece(k, xh, y), z >= k)

            @pl.when(z < k)
            def _():
                mark = lax.broadcasted_iota(jnp.int32, (QUARTER, 128), 1)
                mark = jnp.where((mark >= ROPE) & (mark < ROPE + DOCS), 1.0, 0.0)
                kx[pl.ds(start_of(k, c, xh, y), QUARTER), :] = jnp.concatenate(
                    [jnp.zeros((QUARTER, RANK), F32), mark], axis=1
                ).astype(BF16)

            mine = piece(k, xh, y)
            if k < CHUNKS:
                send(
                    ("z", k + 1), mine, piece(k + 1, xh, y), at((z + 1) % planes, xh, c, y),
                    (z >= k) & (z + 1 < planes),
                )
            send(("x", k, 0), mine, mine, partner, xh == 1 if k == CHUNKS else None)
            for d in (1, 3, 2):
                send(("y", k, d), mine, mine, at(z, xh, c, (y + d) % 4))
            if ROUTES[k] == "S":
                for d in (1, 3, 2):
                    send(("x", k, d), mine, mine, at(z, 1 - xh, c, (y + d) % 4), xh == 1 if k == CHUNKS else None)

        def stage_x(k):
            far = xh == 0 if k == CHUNKS else None
            mine = piece(k, 1 - xh, y)
            arrive(("x", k, 0), mine, far)
            for d in (1, 3, 2):
                send(("y2", k, d), mine, mine, at(z, xh, c, (y + d) % 4), far)

        def stage_xs(k, d):
            mine = piece(k, xh, (y + 4 - d) % 4)
            arrive(("y", k, d), mine)
            send(("x", k, d), mine, mine, partner, xh == 1 if k == CHUNKS else None)

        def stage_ca(k):
            if ROUTES[k] != "X":
                for d in (1, 3, 2):
                    arrive(("y", k, d), piece(k, xh, (y + 4 - d) % 4))
            here = block(k, c, xh)
            send(("ca", k), here, here, twin, c == 1 if k == CHUNKS else None)

        def stage_cb(k):
            far = xh == 0 if k == CHUNKS else None
            if ROUTES[k] == "D":
                for d in (1, 3, 2):
                    arrive(("y2", k, d), piece(k, 1 - xh, (y + 4 - d) % 4), far)
            else:
                for d in range(4):
                    arrive(("x", k, d), piece(k, 1 - xh, (y + 4 - d) % 4 if d else y), far)
            here = block(k, c, 1 - xh)
            if k == CHUNKS:
                arrive("own", here, xh == 1)
            send(("cb", k), here, here, twin)

        def stage_done(k):
            arrive(("ca", k), block(k, 1 - c, xh))
            arrive(("cb", k), block(k, 1 - c, 1 - xh))

        def queries(p):
            base = 3 * 128 * p
            one = qv[:, base : base + 128]
            two = qv[:, base + 128 : base + 256].astype(F32)
            three = qv[:, base + 256 : base + 384].astype(F32)
            two_turned = pltpu.roll(two, 64, 1)
            three_turned = pltpu.roll(three, 64, 1)
            second = jnp.where(lane < 64, two_turned, three_turned).astype(BF16)
            for h, nope, pos in ((2 * p, one, two), (2 * p + 1, second, three_turned)):
                absorbed = lax.dot_general(
                    nope, wk[:, h * NOPE : (h + 1) * NOPE], NT, preferred_element_type=F32
                )
                qx[h * ROWS : (h + 1) * ROWS, 0:RANK] = (absorbed * FOLD).astype(BF16)
                qx[h * ROWS : (h + 1) * ROWS, RANK:WIDE] = jnp.where(lane < ROPE, pos * FOLD, q_mark).astype(BF16)

        def lane_max(scores):
            best = scores[:, 0:128]
            for i in range(1, scores.shape[1] // 128):
                best = jnp.maximum(best, scores[:, i * 128 : (i + 1) * 128])
            return best

        later = lax.broadcasted_iota(jnp.int32, (ROWS, ROWS), 1) > lax.broadcasted_iota(jnp.int32, (ROWS, ROWS), 0)
        causal = jnp.concatenate([jnp.where(later, -2.0 * BIG, 0.0)] * group, axis=0)

        def diagonal(g):
            r = slice(g * grow, (g + 1) * grow)
            scores = lax.dot_general(qx[r, :], kx[0:ROWS, :], NT, preferred_element_type=F32) + causal
            sc[r, 0:ROWS] = scores
            top[r, :] = scores

        def chunk_scores(k, g):
            r = slice(g * grow, (g + 1) * grow)
            first = ROWS + CHUNK * (k - 1)
            scores = lax.dot_general(qx[r, :], kx[first : first + CHUNK, :], NT, preferred_element_type=F32)
            sc[r, first : first + CHUNK] = scores
            best = lane_max(scores)
            if k <= SPLIT:
                top[r, :] = jnp.maximum(top[r, :], best)
            elif k == SPLIT + 1:
                late_top[r, :] = best
            else:
                late_top[r, :] = jnp.maximum(late_top[r, :], best)

        def lane_sum(weights):
            total = weights[:, 0:128]
            for i in range(1, weights.shape[1] // 128):
                total = total + weights[:, i * 128 : (i + 1) * 128]
            return total

        begin = ROWS + CHUNK * SPLIT

        def early(g):
            r = slice(g * grow, (g + 1) * grow)
            high = jnp.max(top[r, :], axis=1, keepdims=True)
            weights = jnp.exp2(sc[r, 0:begin] - high)
            sums[r, :] = lane_sum(weights)
            top[r, :] = jnp.broadcast_to(high, (grow, 128))
            acc[r, :] = jnp.dot(weights.astype(BF16), kx[0:begin, 0:RANK], preferred_element_type=F32)

        wide = 2 * group

        def finish(g):
            r = slice(g * wide * ROWS, (g + 1) * wide * ROWS)
            first = KEYS - CHUNK
            last = lax.dot_general(qx[r, :], kx[first:KEYS, :], NT, preferred_element_type=F32)
            best = lane_max(last)
            if SPLIT < CHUNKS - 1:
                best = jnp.maximum(best, late_top[r, :])
            high = jnp.max(jnp.maximum(best, top[r, :]), axis=1, keepdims=True)
            ratio = jnp.exp2(top[r, :] - high)
            late = jnp.exp2(last - high)
            total = sums[r, :] * ratio + lane_sum(late)
            mixed = acc[r, :] * jnp.concatenate([ratio] * (RANK // 128), axis=1)
            if SPLIT < CHUNKS - 1:
                middle = jnp.exp2(sc[r, begin:first] - high)
                total = total + lane_sum(middle)
                mixed = mixed + jnp.dot(middle.astype(BF16), kx[begin:first, 0:RANK], preferred_element_type=F32)
            mixed = mixed + jnp.dot(late.astype(BF16), kx[first:KEYS, 0:RANK], preferred_element_type=F32)
            total = jnp.sum(total, axis=1, keepdims=True)
            ob[r, :] = (mixed * (1.0 / total)).astype(BF16)
            for h in range(g * wide, (g + 1) * wide):
                att[:, h * VDIM : (h + 1) * VDIM] = jnp.dot(
                    ob[h * ROWS : (h + 1) * ROWS, :],
                    wv[:, h * VDIM : (h + 1) * VDIM],
                    preferred_element_type=F32,
                ).astype(BF16)
            mine = slice(g * wide * VDIM, (g + 1) * wide * VDIM)
            add = lax.dot_general(att[:, mine], wn[:, mine], NT, preferred_element_type=F32)
            if g == 0:
                proj[...] = add
            elif g < heads // wide - 1:
                proj[...] += add
            else:
                total = proj[...] + add
                proj[...] = total
                part[...] = total.astype(BF16)

        send(("z", 1), own_piece, piece(1, xh, y), at((z + 1) % planes, xh, c, y), z + 1 < planes)
        send("own", own, block(CHUNKS, c, xh), partner, xh == 0)
        send(("ca", CHUNKS), own, block(CHUNKS, c, xh), twin, c == 0)
        loads[2].wait()
        loads[3].wait()
        steps = {
            "z": stage_z, "x": stage_x, "xs": stage_xs, "ca": stage_ca, "cb": stage_cb, "done": stage_done,
            "q": queries, "diag": diagonal, "qk": chunk_scores, "early": early,
        }
        for step in PLAN:
            steps[step[0]](*step[1:])
        loads[4].wait()
        loads[5].wait()
        for g in range(heads // wide):
            finish(g)
        store = pltpu.make_async_copy(att, att_hbm, ls.at[6])
        store.start()

        def sixteen(ref, yy, lower):
            return ref.at[pl.ds(pl.multiple_of(yy * QUARTER + lower * HALF, HALF), HALF)]

        for d in range(4):
            to = (y + d) % 4
            send(("rb", d), sixteen(part, to, 1), rsb.at[d], at(z, xh, c, to, 1 - s))
        for d in range(1, 4):
            to = (y + d) % 4
            send(("ra", d), sixteen(part, to, 0), rsa.at[d - 1], beside(to))

        def normal(total):
            low = total[:, 0:RANK]
            inverse = lax.rsqrt(jnp.sum(low * low, axis=1, keepdims=True) * (1.0 / RANK) + 1e-06)
            return (low * inverse).astype(BF16), total[:, RANK:LAT].astype(BF16)

        total = proj[pl.ds(pl.multiple_of(y * QUARTER, QUARTER), HALF), :]
        for d in range(1, 4):
            arrive(("ra", d), rsa.at[d - 1])
            total = total + rsa[d - 1].astype(F32)
        nla[:, 0:RANK], nla[:, RANK:LAT] = normal(total)
        for d in range(4):
            send(("na", d), nla, sixteen(nlb, y, 0), at(z, xh, c, (y + d) % 4, 1 - s))
        total = None
        for d in range(4):
            arrive(("rb", d), rsb.at[d])
            add = rsb[d].astype(F32)
            total = add if total is None else total + add
        lower = pl.ds(pl.multiple_of(y * QUARTER + HALF, HALF), HALF)
        nlb[lower, 0:RANK], nlb[lower, RANK:LAT] = normal(total)
        for d in range(1, 4):
            send(("nb", d), sixteen(nlb, y, 1), sixteen(nlb, y, 1), beside((y + d) % 4))
        for d in range(4):
            arrive(("na", d), sixteen(nlb, (y + 4 - d) % 4, 0))
        for d in range(1, 4):
            arrive(("nb", d), sixteen(nlb, (y + 4 - d) % 4, 1))
        out = pltpu.make_async_copy(nlb, next_hbm, ls.at[7])
        out.start()
        for when, one in sent:
            if when is None:
                one.wait_send()
            else:
                pl.when(when)(one.wait_send)
        store.wait()
        out.wait()

    def call(latent, queries, w_key, w_value, w_next, segments):
        return pl.pallas_call(
            kernel,
            out_shape=(
                jax.ShapeDtypeStruct((ROWS, heads * VDIM), BF16),
                jax.ShapeDtypeStruct((ROWS, LAT), BF16),
            ),
            in_specs=[pl.BlockSpec(memory_space=pl.ANY)] * 6,
            out_specs=[pl.BlockSpec(memory_space=pl.ANY)] * 2,
            scratch_shapes=[
                pltpu.VMEM((LAT, ROWS), BF16),
                pltpu.VMEM((1, ROWS), jnp.int32),
                pltpu.VMEM((ROWS, heads * (NOPE + ROPE)), BF16),
                pltpu.VMEM((RANK, heads * NOPE), BF16),
                pltpu.VMEM((RANK, heads * VDIM), BF16),
                pltpu.VMEM((LAT, heads * VDIM), BF16),
                pltpu.VMEM((rows_all, WIDE), BF16),
                pltpu.VMEM((KEYS, WIDE), BF16),
                pltpu.VMEM((rows_all, KEYS - CHUNK), F32),
                pltpu.VMEM((rows_all, 128), F32),
                pltpu.VMEM((rows_all, 128), F32),
                pltpu.VMEM((rows_all, 128), F32),
                pltpu.VMEM((rows_all, RANK), F32),
                pltpu.VMEM((rows_all, RANK), BF16),
                pltpu.VMEM((ROWS, heads * VDIM), BF16),
                pltpu.VMEM((ROWS, LAT), F32),
                pltpu.VMEM((ROWS, LAT), BF16),
                pltpu.VMEM((3, HALF, LAT), BF16),
                pltpu.VMEM((4, HALF, LAT), BF16),
                pltpu.VMEM((HALF, LAT), BF16),
                pltpu.VMEM((ROWS, LAT), BF16),
                pltpu.SemaphoreType.DMA((8,)),
                pltpu.SemaphoreType.DMA((SEMS,)),
                pltpu.SemaphoreType.DMA((SEMS,)),
            ],
            compiler_params=pltpu.CompilerParams(
                collective_id=0, has_side_effects=True, vmem_limit_bytes=58 * 2**20
            ),
            name="attend",
        )(latent, queries, w_key, w_value, w_next, segments)

    return call


def hand_over(rows, turned, rows_out, turned_out):
    rows_out[0] = rows[...]
    turned_out[0] = turned[...].astype(F32).T.astype(BF16)


def results(rows, turned):
    return pl.pallas_call(
        hand_over,
        out_shape=(
            jax.ShapeDtypeStruct((1,) + rows.shape, BF16),
            jax.ShapeDtypeStruct((1, LAT, ROWS), BF16),
        ),
        name="results",
    )(rows, turned)


def solution(mesh):
    planes = mesh.shape["ctx"] // 4

    def local(latent, queries, w_key, w_value, w_next, segments):
        rows, mixed = make_kernel(planes, w_key.shape[2] // NOPE)(
            jnp.swapaxes(latent, 1, 2), queries, w_key, w_value, jnp.swapaxes(w_next, 1, 2), segments
        )
        attention, turned = results(rows, mixed)
        return attention, jnp.swapaxes(turned, 1, 2)

    in_specs = (
        P("section", "ctx", None),
        P("section", "ctx", "head"),
        P("section", None, "head"),
        P("section", None, "head"),
        P("section", "head", None),
        P("section", "ctx"),
    )
    out_specs = (P("section", "ctx", "head"), P("section", "ctx", None))
    return jax.shard_map(local, mesh=mesh, in_specs=in_specs, out_specs=out_specs, check_vma=False)
```
